1024 devices in a mesh: gx: 16 (over x, z_hi), gy: 8 (over y), gz: 8 (over z_lo, core).
Axes of the slice: x: 8, y: 8, z: 8 (z_hi: 2, z_lo: 4; z = z_hi * 4 + z_lo), core: 2. Of those that a mesh axis runs over, the one named last changes fastest.
Arguments:
- flow_moments: float32 [10, 64, 64, 1024], P(None, 'gx', 'gy', 'gz'), may hold values from -4 to 4
- species_moments: float32 [4, 64, 64, 1024], P(None, 'gx', 'gy', 'gz'), may hold values from -6 to 6
- fluid_mask: int32 [64, 64, 1024], P('gx', 'gy', 'gz'), may hold values from 0 to 1, as said below
- reactive_mask: int32 [64, 64, 1024], P('gx', 'gy', 'gz'), may hold values 0 or 1
Outputs:
- flow_out: float32 [10, 64, 64, 1024], P(None, 'gx', 'gy', 'gz')
- species_out: float32 [4, 64, 64, 1024], P(None, 'gx', 'gy', 'gz')
- dissolved: float32 [64, 64, 1024], P('gx', 'gy', 'gz')
The draws below stay inside these ranges and needn't reach their ends.
Inputs may be any that keep to these rules, and one draw needn't show every extreme that they name: `fluid_mask`: the share of fluid voxels differs from one block of 4 x 8 x 128 voxels to another. `reactive_mask`: read only at solid voxels.
All inputs are finite; a program needn't handle non-finite values. No bound on the sum of `reactive_mask` on one device may be relied on, other than what follows from the above.
Results may differ from the reference program's by a relative error of at most 0.0003.
Values sent between devices are 32-bit elements; how exact they have to be, the bound alone decides.
No kernel may reach another device: no remote copies, remote signals or barrier semaphores. Data moves between devices by JAX's collectives and lax.ppermute only.
A program may use at most 32 MiB of HBM per device.

```python
import jax
import jax.numpy as jnp

CX = 4
CY = 8
CZ = 128
ITERS = 4
NX = 64
NY = 64
NZ = 1024


def draw_fluid_mask(key, part):
    key = jax.random.fold_in(key, 3)
    first, second = jax.random.split(key)
    limits = jax.random.randint(first, (NX // CX, NY // CY, NZ // CZ), 250, 751)
    limits = jnp.repeat(jnp.repeat(jnp.repeat(limits, CX, axis=0), CY, axis=1), CZ, axis=2)
    values = jax.random.randint(second, (NX, NY, NZ), 0, 1000)
    return (values < limits).astype(jnp.int32)


def touch_ends(result, rng, least, top_value):
    place = [jax.random.randint(jax.random.fold_in(rng, axis), (), 0, length) for axis, length in enumerate(result.shape)]
    main_axis = result.shape.index(max(result.shape))
    neighbour = place[:main_axis] + [(place[main_axis] + 1) % result.shape[main_axis]] + place[main_axis + 1:]
    return result.at[tuple(place)].set(least).at[tuple(neighbour)].set(top_value)


def level_of(key, extent, cuts, least, largest):
    def one(dim, shards_of):
        heights = jax.random.uniform(jax.random.fold_in(jax.random.fold_in(key, 6), dim), (shards_of,), jnp.float32, least / len(cuts), largest / len(cuts))
        return jnp.repeat(jnp.exp(heights), extent[dim] // shards_of).reshape((-1,) + (1,) * (len(extent) - dim - 1))

    level = one(*cuts[0])
    for cut in cuts[1:]:
        level = level * one(*cut)
    return level


def noise(rng, extent, deviation, limit, cuts=(), dtype=jnp.bfloat16):
    level = level_of(rng, extent, cuts, -0.22, 0.18) if cuts else 1.0
    array = jax.random.normal(rng, extent, jnp.float32) * deviation * level
    return jnp.minimum(jnp.maximum(array, -limit), limit).astype(dtype)


def setup_inputs(seed: int = 0) -> dict:
    splits = jax.random.split(jax.random.key(seed), 5)
    flow_moments = noise(splits[0], (10, NX, NY, NZ), 0.3, 4.0, ((1, 16), (2, 8), (3, 8)), jnp.float32)
    species_moments = noise(splits[1], (4, NX, NY, NZ), 1.0, 6.0, ((1, 16), (2, 8), (3, 8)), jnp.float32)
    fluid_mask = draw_fluid_mask(jax.random.fold_in(splits[4], 71), 0)
    reactive_mask = touch_ends((jax.random.randint(splits[3], (NX, NY, NZ), 0, 2) < 1).astype(jnp.int32), jax.random.fold_in(splits[3], 1), 0, 1)
    return {"flow_moments": flow_moments, "species_moments": species_moments, "fluid_mask": fluid_mask, "reactive_mask": reactive_mask}


KEEP_FLOW = 1.0 - 1.0 / 0.8
KEEP_SPECIES = 1.0 - 1.0 / 0.7
REACT_RATE = 0.5
SATURATION = 1.0
GRAVITY = 0.001

FLOW_DIRECTIONS = [(0, 0, 0), (1, 0, 0), (-1, 0, 0), (0, 1, 0), (0, -1, 0), (0, 0, 1), (0, 0, -1),
                   (1, 1, 0), (-1, -1, 0), (1, -1, 0), (-1, 1, 0), (1, 0, 1), (-1, 0, -1), (1, 0, -1),
                   (-1, 0, 1), (0, 1, 1), (0, -1, -1), (0, 1, -1), (0, -1, 1)]
FLOW_WEIGHTS = [1.0 / 3.0] + [1.0 / 18.0] * 6 + [1.0 / 36.0] * 12
SPECIES_DIRECTIONS = FLOW_DIRECTIONS[:7]
SPECIES_WEIGHTS = [0.25] + [0.125] * 6


def window(padded, vel, sign):
    size_a = padded.shape[-3] - 2
    size_b = padded.shape[-2] - 2
    size_c = padded.shape[-1] - 2
    start_a = 1 + sign * vel[0]
    start_b = 1 + sign * vel[1]
    start_c = 1 + sign * vel[2]
    return padded[..., start_a:start_a + size_a, start_b:start_b + size_b, start_c:start_c + size_c]


def rebuild_flow(moments, vel, weight):
    rho = moments[0]
    axx = moments[4] - rho / 3.0
    ayy = moments[5] - rho / 3.0
    azz = moments[6] - rho / 3.0
    quad = vel[0] * vel[0] * axx + vel[1] * vel[1] * ayy + vel[2] * vel[2] * azz
    quad = quad + 2.0 * (vel[0] * vel[1] * moments[7] + vel[0] * vel[2] * moments[8] + vel[1] * vel[2] * moments[9])
    quad = quad - (axx + ayy + azz) / 3.0
    lin = vel[0] * moments[1] + vel[1] * moments[2] + vel[2] * moments[3]
    return weight * (rho + 3.0 * lin + 4.5 * quad)


def rebuild_species(moments, vel, weight):
    lin = vel[0] * moments[1] + vel[1] * moments[2] + vel[2] * moments[3]
    return weight * (moments[0] + 4.0 * lin)


def flow_collide(moments, fluid):
    rho = moments[0]
    jx, jy, jz = moments[1], moments[2], moments[3]
    equil = [rho / 3.0 + jx * jx, rho / 3.0 + jy * jy, rho / 3.0 + jz * jz, jx * jy, jx * jz, jy * jz]
    stress = [equil[k] + KEEP_FLOW * (moments[4 + k] - equil[k]) for k in range(6)]
    return jnp.stack([rho, jx, jy, jz] + stress) * fluid


def species_collide(species, flow, fluid):
    conc = species[0]
    fluxes = [conc * flow[1 + k] + KEEP_SPECIES * (species[1 + k] - conc * flow[1 + k]) for k in range(3)]
    return jnp.stack([conc] + fluxes) * fluid


def advance(flow_pad, species_pad, flag_pad, flow_own, species_own, fluid, react, dissolved):
    totals = [jnp.zeros_like(fluid) for k in range(10)]
    for index, vel in enumerate(FLOW_DIRECTIONS):
        weight = FLOW_WEIGHTS[index]
        back = (-vel[0], -vel[1], -vel[2])
        source_fluid = window(flag_pad[0], vel, -1)
        popul = jnp.where(source_fluid > 0.5, rebuild_flow(window(flow_pad, vel, -1), vel, weight),
                          rebuild_flow(flow_own, back, weight))
        coefs = [1, vel[0], vel[1], vel[2], vel[0] * vel[0], vel[1] * vel[1], vel[2] * vel[2],
                 vel[0] * vel[1], vel[0] * vel[2], vel[1] * vel[2]]
        for k in range(10):
            if coefs[k] != 0:
                totals[k] = totals[k] + coefs[k] * popul
    totals[1] = totals[1] + GRAVITY
    new_flow = jnp.stack(totals) * fluid
    sums = [jnp.zeros_like(fluid) for k in range(4)]
    for index, vel in enumerate(SPECIES_DIRECTIONS):
        weight = SPECIES_WEIGHTS[index]
        back = (-vel[0], -vel[1], -vel[2])
        source_fluid = window(flag_pad[0], vel, -1)
        source_react = window(flag_pad[1], vel, -1)
        bounced = rebuild_species(species_own, back, weight)
        reacted = bounced + REACT_RATE * source_react * (weight * SATURATION - bounced)
        popul = jnp.where(source_fluid > 0.5, rebuild_species(window(species_pad, vel, -1), vel, weight), reacted)
        coefs = [1, vel[0], vel[1], vel[2]]
        for k in range(4):
            if coefs[k] != 0:
                sums[k] = sums[k] + coefs[k] * popul
        if index > 0:
            neighbour_fluid = window(flag_pad[0], vel, 1)
            outgoing = rebuild_species(window(species_pad, vel, 1), back, weight)
            release = REACT_RATE * react * (weight * SATURATION - outgoing)
            dissolved = dissolved + jnp.where(neighbour_fluid > 0.5, release, 0.0) * (1.0 - fluid)
    new_species = jnp.stack(sums) * fluid
    return new_flow, new_species, dissolved


def pad_grid(values):
    wrapped = jnp.concatenate([values[:, -1:], values, values[:, :1]], axis=1)
    return jnp.pad(wrapped, ((0, 0), (0, 0), (1, 1), (1, 1)))


def reference(flow_moments, species_moments, fluid_mask, reactive_mask):
    fluid = fluid_mask.astype(jnp.float32)
    react = reactive_mask.astype(jnp.float32)
    flag_pad = pad_grid(jnp.stack([fluid, react]))
    flow, species = flow_moments, species_moments
    dissolved = jnp.zeros_like(fluid)
    for step in range(ITERS):
        flow_own = flow_collide(flow, fluid)
        species_own = species_collide(species, flow_own, fluid)
        flow, species, dissolved = advance(pad_grid(flow_own), pad_grid(species_own), flag_pad,
                                           flow_own, species_own, fluid, react, dissolved)
    return flow, species, dissolved
```

```python
import jax
import jax.numpy as jnp
from jax import lax
from jax.experimental import pallas as pl
from jax.experimental.pallas import tpu as pltpu
from jax.sharding import PartitionSpec as P

STEPS = 4
DEEP = 4
KEEP_FLOW = 1.0 - 1.0 / 0.8
KEEP_SPECIES = 1.0 - 1.0 / 0.7
REACT_RATE = 0.5
GRAVITY = 0.001
MOVING = [
    (1, 0, 0),
    (-1, 0, 0),
    (0, 1, 0),
    (0, -1, 0),
    (0, 0, 1),
    (0, 0, -1),
    (1, 1, 0),
    (-1, -1, 0),
    (1, -1, 0),
    (-1, 1, 0),
    (1, 0, 1),
    (-1, 0, -1),
    (1, 0, -1),
    (-1, 0, 1),
    (0, 1, 1),
    (0, -1, -1),
    (0, 1, -1),
    (0, -1, 1),
]
NFLOW = 18
NSPEC = 6
SPECIES_WEIGHT = 0.125
INPLANE = [(0, 0), (1, 0), (-1, 0), (0, 1), (0, -1), (1, 1), (-1, -1), (1, -1), (-1, 1)]
PLANE_OF = {shift: place for place, shift in enumerate(INPLANE)}
FIELDS = 15
FLUID = 14
ROWS = 8
LANES = 128


def opposite(index):
    return index ^ 1


def flow_populations(m):
    third = m[0] * (1.0 / 3.0)
    axx, ayy, azz = m[4] - third, m[5] - third, m[6] - third
    base = m[0] - 1.5 * (axx + ayy + azz)
    sides = (4.5 * axx, 4.5 * ayy, 4.5 * azz)
    drift = [m[1 + k] * (1.0 / 12.0) for k in range(3)]
    moving = []
    lifted = [base + side for side in sides]
    for k in range(3):
        even, odd = lifted[k] * (1.0 / 18.0), m[1 + k] * (1.0 / 6.0)
        moving += [even + odd, even - odd]
    for a, b, cross in ((0, 1, 7), (0, 2, 8), (1, 2, 9)):
        both = (lifted[a] + sides[b]) * (1.0 / 36.0)
        mixed = m[cross] * 0.25
        same, differ = both + mixed, both - mixed
        plus, minus = drift[a] + drift[b], drift[a] - drift[b]
        moving += [same + plus, same - plus, differ + minus, differ - minus]
    return base * (1.0 / 3.0), moving


def species_populations(s):
    part = s[0] * SPECIES_WEIGHT
    moving = []
    for k in range(3):
        odd = s[1 + k] * 0.5
        moving += [part + odd, part - odd]
    return s[0] * 0.25, moving


def collide(flow, species):
    rho = flow[0]
    j = flow[1:4]
    third = rho * (1.0 / 3.0)
    equil = [third + j[0] * j[0], third + j[1] * j[1], third + j[2] * j[2], j[0] * j[1], j[0] * j[2], j[1] * j[2]]
    stress = [KEEP_FLOW * flow[4 + k] + (1.0 - KEEP_FLOW) * equil[k] for k in range(6)]
    conc = species[0]
    flux = [KEEP_SPECIES * species[1 + k] + (1.0 - KEEP_SPECIES) * (conc * j[k]) for k in range(3)]
    return [rho] + list(j) + stress + [conc] + flux


def pass_on(post, arriving, flags, arriving_species, slow, fluid):
    rest, own = flow_populations(post[:10])
    f = [jnp.where(flags(c) > 0.5, arriving(c), own[opposite(c)]) for c in range(NFLOW)]
    total = [f[2 * k] + f[2 * k + 1] for k in range(9)]
    diff = [f[2 * k] - f[2 * k + 1] for k in range(9)]
    xy, xz, yz = total[3] + total[4], total[5] + total[6], total[7] + total[8]
    rho = rest + (total[0] + total[1] + total[2]) + (xy + xz + yz)
    jx = diff[0] + (diff[3] + diff[4]) + (diff[5] + diff[6]) + GRAVITY
    jy = diff[1] + (diff[3] - diff[4]) + (diff[7] + diff[8])
    jz = diff[2] + (diff[5] - diff[6]) + (diff[7] - diff[8])
    flow = [
        rho,
        jx,
        jy,
        jz,
        total[0] + xy + xz,
        total[1] + xy + yz,
        total[2] + xz + yz,
        total[3] - total[4],
        total[5] - total[6],
        total[7] - total[8],
    ]
    flow = [value * fluid for value in flow]
    rest, own = species_populations(post[10:14])
    g = []
    for c in range(NSPEC):
        back = own[opposite(c)]
        g.append(jnp.where(flags(c) > 0.5, arriving_species(c), back + slow(c) * (SPECIES_WEIGHT - back)))
    conc = rest + (g[0] + g[1]) + (g[2] + g[3]) + (g[4] + g[5])
    species = [conc, g[0] - g[1], g[2] - g[3], g[4] - g[5]]
    return flow, [value * fluid for value in species]


def lanes_of(shape):
    return lax.broadcasted_iota(jnp.int32, shape, len(shape) - 1)


def rows_of(shape):
    return lax.broadcasted_iota(jnp.int32, shape, len(shape) - 2)


def roll(value, shift, axis):
    size = value.shape[axis]
    if isinstance(shift, int):
        shift = shift % size
        if shift == 0:
            return value
    return pltpu.roll(value, shift, axis)


def edge_lanes(layers, field):
    shape = layers[0].shape
    slot = lanes_of(shape) // 8
    first = 4 * (field % 4)
    out = jnp.zeros(shape, jnp.float32)
    for x, layer in enumerate(layers):
        out = jnp.where(slot == first + x, roll(layer, 8 * (first + x) + 4, len(shape) - 1), out)
    return out


def start_kernel(flow_ref, species_ref, fluid_ref, react_ref, block_ref, edge_ref):
    for x in range(DEEP):
        fluid = fluid_ref[x].astype(jnp.float32)
        react = react_ref[x].astype(jnp.float32)
        flow = [flow_ref[k, x] * fluid for k in range(10)]
        species = [species_ref[k, x] * fluid for k in range(4)]
        post = collide(flow, species)
        block_ref[0, x] = jnp.where(fluid > 0.5, post[0], react)
        for k in range(1, 14):
            block_ref[k, x] = post[k]
        block_ref[FLUID, x] = fluid
    for tile in range(4):
        packed = jnp.zeros((ROWS, LANES), jnp.float32)
        for field in range(4 * tile, min(4 * tile + 4, FIELDS)):
            packed = packed + edge_lanes([block_ref[field, x] for x in range(DEEP)], field)
        edge_ref[tile] = packed


def rows_kernel(own_ref, left_ref, right_ref, strip_ref, strip_left_ref, strip_right_ref, up_ref, down_ref):
    high = rows_of((ROWS, LANES)) >= 4

    def put(place, one, two):
        two = roll(two, 4, 0)
        up_ref[place] = jnp.where(high, one, two)
        down_ref[place] = jnp.where(high, two, one)

    layers = [(ref, x) for ref in (left_ref, own_ref, right_ref) for x in range(DEEP)]
    for field in range(FIELDS):
        for k in range(6):
            (one, a), (two, b) = layers[k], layers[k + 6]
            put(field * 6 + k, one[field, a], two[field, b])
    tiles = [(ref, t) for ref in (strip_left_ref, strip_ref, strip_right_ref) for t in range(4)]
    for k in range(6):
        (one, a), (two, b) = tiles[k], tiles[k + 6]
        put(FIELDS * 6 + k, one[a], two[b])


def steps_kernel(
    own_ref,
    left_ref,
    right_ref,
    strip_ref,
    strip_left_ref,
    strip_right_ref,
    up_ref,
    down_ref,
    flow_out,
    species_out,
    dissolved_out,
    state,
    fluid_at,
    slow_at,
    sent,
    halo,
    strips,
    strip_fluid,
    strip_slow,
    strip_sent,
    released,
):
    tall = (2 * ROWS, LANES)
    low_rows = rows_of((ROWS, LANES)) < 4
    lane = lanes_of(tall)
    slot_lane = lanes_of((ROWS, LANES)) % 8
    blocks = (left_ref, own_ref, right_ref)

    def halves(place):
        up, down = up_ref[place], down_ref[place]
        return jnp.where(low_rows, down, up), roll(jnp.where(low_rows, up, down), 4, 0)

    for field in range(FIELDS):
        for x in range(12):
            state[field, x, 0:ROWS] = blocks[x // 4][field, x % 4]
        for k in range(6):
            one, two = halves(field * 6 + k)
            state[field, k, ROWS : 2 * ROWS] = one
            state[field, k + 6, ROWS : 2 * ROWS] = two
    strip_blocks = (strip_left_ref, strip_ref, strip_right_ref)
    for place in range(12):
        halo[place, 0:ROWS] = strip_blocks[place // 4][place % 4]
    for k in range(6):
        one, two = halves(FIELDS * 6 + k)
        halo[k, ROWS : 2 * ROWS] = one
        halo[k + 6, ROWS : 2 * ROWS] = two

    inner = lanes_of(tall) % 8 < 4
    group = lanes_of(tall) // 32
    for field in range(FIELDS):
        low = jnp.zeros(tall, jnp.float32)
        far = jnp.zeros(tall, jnp.float32)
        for b, target in ((0, 3), (1, 0), (2, 1)):
            edge = edge_lanes([state[field, 4 * b + x] for x in range(DEEP)], 0)
            edge = roll(edge, 32 * target, 1)
            beyond = roll(halo[4 * b + field // 4], 32 * ((target - field % 4) % 4), 1)
            here = group == target
            low = jnp.where(here, jnp.where(inner, beyond, edge), low)
            far = jnp.where(here, jnp.where(inner, edge, beyond), far)
        strips[0, field] = low
        strips[1, field] = far

    def split_first(value, fluid):
        return value * fluid, REACT_RATE * value * (1.0 - fluid)

    def strip_moved(value, c):
        cx, cy, cz = MOVING[c]
        return roll(roll(value, 8 * cx + cz, 1), cy, 0)

    strip_slow_here = []
    for side in range(2):
        fluid = strips[side, FLUID]
        rho, slow = split_first(strips[side, 0], fluid)
        strips[side, 0] = rho
        strip_slow_here.append(slow)
        for c in range(NFLOW):
            strip_fluid[side, c] = strip_moved(fluid, c)
        for c in range(NSPEC):
            strip_slow[side, c] = strip_moved(slow, c)

    def from_strip(value, x, cz):
        slot = lax.rem(x + 12, 16)
        if cz > 0:
            return pltpu.roll(value, lax.rem(125 + 128 - 8 * slot, 128), 1)
        return pltpu.roll(value, lax.rem(123 + 128 - 8 * slot, 128), 1)

    def moved(value, x, cy, cz, strip_value):
        if cz > 0:
            value = jnp.where(lane == 0, from_strip(strip_value, x, 1), roll(value, 1, 1))
        elif cz < 0:
            value = jnp.where(lane == LANES - 1, from_strip(strip_value, x, -1), roll(value, -1, 1))
        return roll(value, cy, 0)

    def side_of(cz):
        return 0 if cz > 0 else 1

    def flags_at(x, carry):
        fluid = state[FLUID, x]
        rho, slow = split_first(state[0, x], fluid)
        state[0, x] = rho
        for place, (cy, cz) in enumerate(INPLANE):
            fluid_at[place, x] = moved(fluid, x, cy, cz, strips[side_of(cz), FLUID])
            if place < 5:
                slow_at[place, x] = moved(slow, x, cy, cz, strip_slow_here[side_of(cz)])
        return carry

    lax.fori_loop(0, 12, flags_at, 0)
    for x in range(DEEP, 2 * DEEP):
        released[x] = jnp.zeros((ROWS, LANES), jnp.float32)

    for step in range(STEPS):
        last = step == STEPS - 1
        for side in range(2):
            post = [strips[side, k] for k in range(14)]
            _, flow_pops = flow_populations(post[:10])
            _, species_pops = species_populations(post[10:])
            for c in range(NFLOW):
                if MOVING[c][2] == (1, -1)[side]:
                    strip_sent[c] = flow_pops[c]
                    if c < NSPEC:
                        strip_sent[NFLOW + c] = species_pops[c]
            if not last:
                new_flow, new_species = pass_on(
                    post,
                    lambda c: strip_moved(flow_pops[c], c),
                    lambda c: strip_fluid[side, c],
                    lambda c: strip_moved(species_pops[c], c),
                    lambda c: strip_slow[side, c],
                    strips[side, FLUID],
                )
                for k, value in enumerate(collide(new_flow, new_species)):
                    strips[side, k] = value

        def send(x, carry):
            _, flow_pops = flow_populations([state[k, x] for k in range(10)])
            _, species_pops = species_populations([state[k, x] for k in range(10, 14)])
            for c in range(NFLOW):
                _, cy, cz = MOVING[c]
                sent[c, x] = moved(flow_pops[c], x, cy, cz, strip_sent[c] if cz else None)
            for c in range(NSPEC):
                _, cy, cz = MOVING[c]
                sent[NFLOW + c, x] = moved(species_pops[c], x, cy, cz, strip_sent[NFLOW + c] if cz else None)
            return carry

        lax.fori_loop(step, 12 - step, send, 0)
        height = ROWS if last else 2 * ROWS

        def receive(x, carry):
            def at(ref, place, c):
                return ref[place, x - MOVING[c][0], 0:height]

            post = [state[k, x, 0:height] for k in range(14)]
            new_flow, new_species = pass_on(
                post,
                lambda c: at(sent, c, c),
                lambda c: at(fluid_at, PLANE_OF[MOVING[c][1:]], c),
                lambda c: at(sent, NFLOW + c, c),
                lambda c: at(slow_at, PLANE_OF[MOVING[c][1:]], c),
                state[FLUID, x, 0:height],
            )
            if last:
                for k in range(10):
                    flow_out[k, x - DEEP] = new_flow[k]
                for k in range(4):
                    species_out[k, x - DEEP] = new_species[k]
            else:
                for k, value in enumerate(collide(new_flow, new_species)):
                    state[k, x] = value
            return carry

        lax.fori_loop(step + 1, 11 - step, receive, 0)

        def release(x, carry):
            parts = [sent[NFLOW + c, x - MOVING[c][0], 0:ROWS] for c in range(NSPEC)]
            released[x] = released[x] + ((parts[0] + parts[1]) + (parts[2] + parts[3]) + (parts[4] + parts[5]))
            return carry

        lax.fori_loop(DEEP, 2 * DEEP, release, 0)

    for x in range(DEEP, 2 * DEEP):
        near = [fluid_at[PLANE_OF[MOVING[c][1:]], x - MOVING[c][0], 0:ROWS] for c in range(NSPEC)]
        count = (near[0] + near[1]) + (near[2] + near[3]) + (near[4] + near[5])
        slow = slow_at[PLANE_OF[(0, 0)], x, 0:ROWS]
        dissolved_out[x - DEEP] = slow * (STEPS * SPECIES_WEIGHT * count - released[x])


def shifted(value, axis, wrap):
    count = lax.axis_size(axis)
    up = [(i, (i + 1) % count) for i in range(count if wrap else count - 1)]
    down = [(j, i) for i, j in up]
    return lax.ppermute(value, axis, up), lax.ppermute(value, axis, down)


def vmem(count):
    return [pl.BlockSpec(memory_space=pltpu.VMEM)] * count


def per_device(flow_moments, species_moments, fluid_mask, reactive_mask):
    f32 = jnp.float32
    params = pltpu.CompilerParams(vmem_limit_bytes=24 * 1024 * 1024)
    block, edge = pl.pallas_call(
        start_kernel,
        out_shape=(
            jax.ShapeDtypeStruct((FIELDS, DEEP, ROWS, LANES), f32),
            jax.ShapeDtypeStruct((4, ROWS, LANES), f32),
        ),
        in_specs=vmem(4),
        out_specs=tuple(vmem(2)),
        compiler_params=params,
    )(flow_moments, species_moments, fluid_mask, reactive_mask)
    left, right = shifted(block, "gx", True)
    below, above = shifted(edge, "gz", False)
    strip = jnp.where(lanes_of(edge.shape) % 8 < 4, below, above)
    strip_left, strip_right = shifted(strip, "gx", True)
    tiles = jax.ShapeDtypeStruct((FIELDS * 6 + 6, ROWS, LANES), f32)
    to_up, to_down = pl.pallas_call(
        rows_kernel,
        out_shape=(tiles, tiles),
        in_specs=vmem(6),
        out_specs=tuple(vmem(2)),
        compiler_params=params,
    )(block, left, right, strip, strip_left, strip_right)
    count = lax.axis_size("gy")
    from_low = lax.ppermute(to_up, "gy", [(i, i + 1) for i in range(count - 1)])
    from_high = lax.ppermute(to_down, "gy", [(i + 1, i) for i in range(count - 1)])
    tall = (2 * ROWS, LANES)
    return pl.pallas_call(
        steps_kernel,
        out_shape=(
            jax.ShapeDtypeStruct(flow_moments.shape, f32),
            jax.ShapeDtypeStruct(species_moments.shape, f32),
            jax.ShapeDtypeStruct(fluid_mask.shape, f32),
        ),
        in_specs=vmem(8),
        out_specs=tuple(vmem(3)),
        scratch_shapes=[
            pltpu.VMEM((FIELDS, 12) + tall, f32),
            pltpu.VMEM((9, 12) + tall, f32),
            pltpu.VMEM((5, 12) + tall, f32),
            pltpu.VMEM((NFLOW + NSPEC, 12) + tall, f32),
            pltpu.VMEM((12,) + tall, f32),
            pltpu.VMEM((2, FIELDS) + tall, f32),
            pltpu.VMEM((2, NFLOW) + tall, f32),
            pltpu.VMEM((2, NSPEC) + tall, f32),
            pltpu.VMEM((NFLOW + NSPEC,) + tall, f32),
            pltpu.VMEM((12, ROWS, LANES), f32),
        ],
        compiler_params=params,
    )(block, left, right, strip, strip_left, strip_right, from_low, from_high)


def solution(mesh):
    return jax.shard_map(
        per_device,
        mesh=mesh,
        in_specs=(
            P(None, "gx", "gy", "gz"),
            P(None, "gx", "gy", "gz"),
            P("gx", "gy", "gz"),
            P("gx", "gy", "gz"),
        ),
        out_specs=(P(None, "gx", "gy", "gz"), P(None, "gx", "gy", "gz"), P("gx", "gy", "gz")),
        check_vma=False,
    )
```

```python
import jax
import jax.numpy as jnp
from jax import lax
from jax.experimental import pallas as pl
from jax.experimental.pallas import tpu as pltpu
from jax.sharding import PartitionSpec as P

STEPS = 4
DEEP = 4
KEEP_FLOW = 1.0 - 1.0 / 0.8
KEEP_SPECIES = 1.0 - 1.0 / 0.7
REACT_RATE = 0.5
GRAVITY = 0.001
MOVING = [
    (1, 0, 0),
    (-1, 0, 0),
    (0, 1, 0),
    (0, -1, 0),
    (0, 0, 1),
    (0, 0, -1),
    (1, 1, 0),
    (-1, -1, 0),
    (1, -1, 0),
    (-1, 1, 0),
    (1, 0, 1),
    (-1, 0, -1),
    (1, 0, -1),
    (-1, 0, 1),
    (0, 1, 1),
    (0, -1, -1),
    (0, 1, -1),
    (0, -1, 1),
]
NFLOW = 18
NSPEC = 6
SPECIES_WEIGHT = 0.125
FIELDS = 15
FLUID = 14
ROWS = 8
LANES = 128
SOLID = float("nan")
REACTIVE = float("inf")
LARGEST = 3.0e38


def opposite(index):
    return index ^ 1


def flow_populations(m):
    third = m[0] * (1.0 / 3.0)
    axx, ayy, azz = m[4] - third, m[5] - third, m[6] - third
    base = m[0] - 1.5 * (axx + ayy + azz)
    sides = (4.5 * axx, 4.5 * ayy, 4.5 * azz)
    drift = [m[1 + k] * (1.0 / 12.0) for k in range(3)]
    moving = []
    lifted = [base + side for side in sides]
    for k in range(3):
        even, odd = lifted[k] * (1.0 / 18.0), m[1 + k] * (1.0 / 6.0)
        moving += [even + odd, even - odd]
    for a, b, cross in ((0, 1, 7), (0, 2, 8), (1, 2, 9)):
        both = (lifted[a] + sides[b]) * (1.0 / 36.0)
        mixed = m[cross] * 0.25
        same, differ = both + mixed, both - mixed
        plus, minus = drift[a] + drift[b], drift[a] - drift[b]
        moving += [same + plus, same - plus, differ + minus, differ - minus]
    return base * (1.0 / 3.0), moving


def species_populations(s):
    part = s[0] * SPECIES_WEIGHT
    moving = []
    for k in range(3):
        odd = s[1 + k] * 0.5
        moving += [part + odd, part - odd]
    return s[0] * 0.25, moving


def collide(flow, species):
    rho = flow[0]
    j = flow[1:4]
    third = rho * (1.0 / 3.0)
    equil = [third + j[0] * j[0], third + j[1] * j[1], third + j[2] * j[2], j[0] * j[1], j[0] * j[2], j[1] * j[2]]
    stress = [KEEP_FLOW * flow[4 + k] + (1.0 - KEEP_FLOW) * equil[k] for k in range(6)]
    conc = species[0]
    flux = [KEEP_SPECIES * species[1 + k] + (1.0 - KEEP_SPECIES) * (conc * j[k]) for k in range(3)]
    return [rho] + list(j) + stress + [conc] + flux


def is_number(value):
    return value < LARGEST


def pass_on(post, arriving, arriving_species):
    rest, own = flow_populations(post[:10])
    f = []
    for c in range(NFLOW):
        value = arriving(c)
        f.append(jnp.where(is_number(value), value, own[opposite(c)]))
    total = [f[2 * k] + f[2 * k + 1] for k in range(9)]
    diff = [f[2 * k] - f[2 * k + 1] for k in range(9)]
    xy, xz, yz = total[3] + total[4], total[5] + total[6], total[7] + total[8]
    rho = rest + (total[0] + total[1] + total[2]) + (xy + xz + yz)
    jx = diff[0] + (diff[3] + diff[4]) + (diff[5] + diff[6]) + GRAVITY
    jy = diff[1] + (diff[3] - diff[4]) + (diff[7] + diff[8])
    jz = diff[2] + (diff[5] - diff[6]) + (diff[7] - diff[8])
    flow = [
        rho,
        jx,
        jy,
        jz,
        total[0] + xy + xz,
        total[1] + xy + yz,
        total[2] + xz + yz,
        total[3] - total[4],
        total[5] - total[6],
        total[7] - total[8],
    ]
    rest, own = species_populations(post[10:14])
    g = []
    for c in range(NSPEC):
        value = arriving_species(c)
        back = own[opposite(c)]
        slow = jnp.where(value > LARGEST, REACT_RATE, 0.0)
        g.append(jnp.where(is_number(value), value, back + slow * (SPECIES_WEIGHT - back)))
    conc = rest + (g[0] + g[1]) + (g[2] + g[3]) + (g[4] + g[5])
    return flow, [conc, g[0] - g[1], g[2] - g[3], g[4] - g[5]]


def next_post(post, flow, species):
    fluid = is_number(post[0])
    new = collide(flow, species)
    new[0] = jnp.where(fluid, new[0], post[0])
    new[10] = jnp.where(fluid, new[10], post[10])
    for k in range(11, 14):
        new[k] = jnp.where(fluid, new[k], 0.0)
    return new


def lanes_of(shape):
    return lax.broadcasted_iota(jnp.int32, shape, len(shape) - 1)


def rows_of(shape):
    return lax.broadcasted_iota(jnp.int32, shape, len(shape) - 2)


def roll(value, shift, axis):
    size = value.shape[axis]
    if isinstance(shift, int):
        shift = shift % size
        if shift == 0:
            return value
    return pltpu.roll(value, shift, axis)


def first_slot():
    return 4 * lax.rem(lax.axis_index("gx"), 4)


def start_kernel(flow_in, species_in, fluid_in, react_in, block_ref, edge_ref, flow_ref, species_ref, fluid_ref, react_ref, done):
    pairs = ((flow_in, flow_ref), (species_in, species_ref), (fluid_in, fluid_ref), (react_in, react_ref))
    copies = [pltpu.make_async_copy(one, two, done.at[k]) for k, (one, two) in enumerate(pairs)]
    for copy in copies:
        copy.start()
    for copy in copies:
        copy.wait()
    slot_of = lanes_of((ROWS, LANES)) // 8
    edges = [jnp.zeros((ROWS, LANES), jnp.float32)] * FIELDS
    for x in range(DEEP):
        slot = first_slot() + x
        fluid = fluid_ref[x].astype(jnp.float32)
        react = react_ref[x].astype(jnp.float32)
        flow = [flow_ref[k, x] * fluid for k in range(10)]
        species = [species_ref[k, x] * fluid for k in range(4)]
        post = collide(flow, species)
        post[0] = jnp.where(fluid > 0.5, post[0], react)
        for k, value in enumerate(post + [fluid]):
            value = roll(value, 8 * slot + 4, 1)
            block_ref[k, x] = value
            edges[k] = jnp.where(slot_of == slot, value, edges[k])
    for tile in range(4):
        packed = jnp.zeros((ROWS, LANES), jnp.float32)
        for field in range(4 * tile, min(4 * tile + 4, FIELDS)):
            packed = packed + roll(edges[field], 32 * (field % 4), 1)
        edge_ref[tile] = packed


def join_kernel(below_ref, above_ref, block_in, strip_ref, block_ref, done):
    copy = pltpu.make_async_copy(block_in, block_ref, done)
    copy.start()
    for tile in range(4):
        strip_ref[tile] = jnp.where(lanes_of((ROWS, LANES)) % 8 < 4, below_ref[tile], above_ref[tile])
    copy.wait()


def put_rows(up_ref, down_ref, place, one, two):
    high = rows_of((ROWS, LANES)) >= 4
    two = roll(two, 4, 0)
    up_ref[place] = jnp.where(high, one, two)
    down_ref[place] = jnp.where(high, two, one)


def rows_kernel(own_ref, left_ref, right_ref, up_ref, down_ref):
    layers = [(ref, x) for ref in (left_ref, own_ref, right_ref) for x in range(DEEP)]
    for field in range(FIELDS):
        for k in range(6):
            (one, a), (two, b) = layers[k], layers[k + 6]
            put_rows(up_ref, down_ref, field * 6 + k, one[field, a], two[field, b])


def strip_rows_kernel(up_in, down_in, strip_ref, strip_left_ref, strip_right_ref, up_ref, down_ref):
    tiles = [(ref, t) for ref in (strip_left_ref, strip_ref, strip_right_ref) for t in range(4)]
    for k in range(6):
        (one, a), (two, b) = tiles[k], tiles[k + 6]
        put_rows(up_ref, down_ref, FIELDS * 6 + k, one[a], two[b])


def steps_kernel(
    own_ref,
    left_ref,
    right_ref,
    strip_ref,
    strip_left_ref,
    strip_right_ref,
    up_ref,
    down_ref,
    flow_out,
    species_out,
    dissolved_out,
    state,
    sent,
    halo,
    strips,
    strip_sent,
    released,
):
    tall = (2 * ROWS, LANES)
    low_rows = rows_of((ROWS, LANES)) < 4
    lane = lanes_of(tall)
    blocks = (left_ref, own_ref, right_ref)

    def halves(place):
        up, down = up_ref[place], down_ref[place]
        return jnp.where(low_rows, down, up), roll(jnp.where(low_rows, up, down), 4, 0)

    for field in range(FIELDS):
        for x in range(12):
            state[field, x, 0:ROWS] = blocks[x // 4][field, x % 4]
        for k in range(6):
            one, two = halves(field * 6 + k)
            state[field, k, ROWS : 2 * ROWS] = one
            state[field, k + 6, ROWS : 2 * ROWS] = two
    strip_blocks = (strip_left_ref, strip_ref, strip_right_ref)
    for place in range(12):
        halo[place, 0:ROWS] = strip_blocks[place // 4][place % 4]
    for k in range(6):
        one, two = halves(FIELDS * 6 + k)
        halo[k, ROWS : 2 * ROWS] = one
        halo[k + 6, ROWS : 2 * ROWS] = two

    inner = lane % 8 < 4

    def slot_at(x):
        return lax.rem(first_slot() + x + 12, 16)

    for field in range(FIELDS):
        edge = jnp.zeros(tall, jnp.float32)
        beyond = jnp.zeros(tall, jnp.float32)
        for x in range(12):
            edge = jnp.where(lane // 8 == slot_at(x), state[field, x], edge)
        for b in range(3):
            turned = roll(halo[4 * b + field // 4], -32 * (field % 4), 1)
            beyond = jnp.where(lane // 32 == slot_at(4 * b) // 4, turned, beyond)
        strips[0, field] = jnp.where(inner, beyond, edge)
        strips[1, field] = jnp.where(inner, edge, beyond)

    def marked(first, conc, fluid):
        solid = fluid < 0.5
        mark = jnp.where(first > 0.5, REACTIVE, SOLID)
        return jnp.where(solid, SOLID, first), jnp.where(solid, mark, conc)

    for side in range(2):
        rho, conc = marked(strips[side, 0], strips[side, 10], strips[side, FLUID])
        strips[side, 0] = rho
        strips[side, 10] = conc
    for x in range(12):
        rho, conc = marked(state[0, x], state[10, x], state[FLUID, x])
        state[0, x] = rho
        state[10, x] = conc

    def strip_moved(value, c):
        cx, cy, cz = MOVING[c]
        return roll(roll(value, 8 * cx + cz, 1), cy, 0)

    def moved(value, x, c, strip_value):
        cz = MOVING[c][2]
        if cz:
            end = 8 * slot_at(x) + (3 if cz > 0 else 4)
            value = jnp.where(lane == end, strip_value, value)
        return strip_moved(value, c)

    def turned_back(value, x):
        return roll(value, 124 - 8 * slot_at(x), 1)

    for x in range(DEEP, 2 * DEEP):
        released[x] = jnp.zeros((ROWS, LANES), jnp.float32)

    for step in range(STEPS):
        last = step == STEPS - 1
        for side in range(2):
            post = [strips[side, k] for k in range(14)]
            _, flow_pops = flow_populations(post[:10])
            _, species_pops = species_populations(post[10:])
            for c in range(NFLOW):
                if MOVING[c][2] == (1, -1)[side]:
                    strip_sent[c] = flow_pops[c]
                    if c < NSPEC:
                        strip_sent[NFLOW + c] = species_pops[c]
            if not last:
                new_flow, new_species = pass_on(
                    post,
                    lambda c: strip_moved(flow_pops[c], c),
                    lambda c: strip_moved(species_pops[c], c),
                )
                for k, value in enumerate(next_post(post, new_flow, new_species)):
                    strips[side, k] = value

        def send(x):
            _, flow_pops = flow_populations([state[k, x] for k in range(10)])
            _, species_pops = species_populations([state[k, x] for k in range(10, 14)])
            for c in range(NFLOW):
                sent[c, x] = moved(flow_pops[c], x, c, strip_sent[c] if MOVING[c][2] else None)
            for c in range(NSPEC):
                sent[NFLOW + c, x] = moved(species_pops[c], x, c, strip_sent[NFLOW + c] if MOVING[c][2] else None)

        for x in range(step, 12 - step):
            send(x)
        height = ROWS if last else 2 * ROWS

        def receive(x):
            post = [state[k, x, 0:height] for k in range(14)]
            new_flow, new_species = pass_on(
                post,
                lambda c: sent[c, x - MOVING[c][0], 0:height],
                lambda c: sent[NFLOW + c, x - MOVING[c][0], 0:height],
            )
            if last:
                fluid = is_number(post[0])
                for k in range(10):
                    flow_out[k, x - DEEP] = turned_back(jnp.where(fluid, new_flow[k], 0.0), x)
                for k in range(4):
                    species_out[k, x - DEEP] = turned_back(jnp.where(fluid, new_species[k], 0.0), x)
            else:
                for k, value in enumerate(next_post(post, new_flow, new_species)):
                    state[k, x] = value

        for x in range(step + 1, 11 - step):
            receive(x)

        for x in range(DEEP, 2 * DEEP):
            parts = [sent[NFLOW + c, x - MOVING[c][0], 0:ROWS] for c in range(NSPEC)]
            parts = [jnp.where(is_number(part), SPECIES_WEIGHT - part, 0.0) for part in parts]
            released[x] = released[x] + ((parts[0] + parts[1]) + (parts[2] + parts[3]) + (parts[4] + parts[5]))

    for x in range(DEEP, 2 * DEEP):
        reactive = state[10, x, 0:ROWS] > LARGEST
        dissolved_out[x - DEEP] = turned_back(jnp.where(reactive, REACT_RATE * released[x], 0.0), x)


def shifted(value, axis, wrap):
    count = lax.axis_size(axis)
    up = [(i, (i + 1) % count) for i in range(count if wrap else count - 1)]
    down = [(j, i) for i, j in up]
    return lax.ppermute(value, axis, up), lax.ppermute(value, axis, down)


def vmem(count):
    return [pl.BlockSpec(memory_space=pltpu.VMEM)] * count


def per_device(flow_moments, species_moments, fluid_mask, reactive_mask):
    f32 = jnp.float32
    params = pltpu.CompilerParams(vmem_limit_bytes=24 * 1024 * 1024)
    block, edge = pl.pallas_call(
        start_kernel,
        out_shape=(
            jax.ShapeDtypeStruct((FIELDS, DEEP, ROWS, LANES), f32),
            jax.ShapeDtypeStruct((4, ROWS, LANES), f32),
        ),
        in_specs=[pl.BlockSpec(memory_space=pltpu.HBM)] * 4,
        out_specs=tuple(vmem(2)),
        scratch_shapes=[
            pltpu.VMEM(flow_moments.shape, f32),
            pltpu.VMEM(species_moments.shape, f32),
            pltpu.VMEM(fluid_mask.shape, fluid_mask.dtype),
            pltpu.VMEM(reactive_mask.shape, reactive_mask.dtype),
            pltpu.SemaphoreType.DMA((4,)),
        ],
        compiler_params=pltpu.CompilerParams(vmem_limit_bytes=56 * 1024 * 1024),
    )(flow_moments, species_moments, fluid_mask, reactive_mask)
    left, right = shifted(block, "gx", True)
    below, above = shifted(edge, "gz", False)
    strip, block = pl.pallas_call(
        join_kernel,
        out_shape=(jax.ShapeDtypeStruct(edge.shape, f32), jax.ShapeDtypeStruct(block.shape, f32)),
        in_specs=vmem(2) + [pl.BlockSpec(memory_space=pltpu.HBM)],
        out_specs=tuple(vmem(2)),
        scratch_shapes=[pltpu.SemaphoreType.DMA],
        compiler_params=params,
        cost_estimate=pl.CostEstimate(flops=1, bytes_accessed=1, transcendentals=0),
    )(below, above, block)
    strip_left, strip_right = shifted(strip, "gx", True)
    tiles = jax.ShapeDtypeStruct((FIELDS * 6 + 6, ROWS, LANES), f32)
    to_up, to_down = pl.pallas_call(
        rows_kernel,
        out_shape=(tiles, tiles),
        in_specs=vmem(3),
        out_specs=tuple(vmem(2)),
        compiler_params=params,
        cost_estimate=pl.CostEstimate(flops=10**11, bytes_accessed=10**8, transcendentals=0),
    )(block, left, right)
    to_up, to_down = pl.pallas_call(
        strip_rows_kernel,
        out_shape=(tiles, tiles),
        in_specs=vmem(5),
        out_specs=tuple(vmem(2)),
        input_output_aliases={0: 0, 1: 1},
        compiler_params=params,
    )(to_up, to_down, strip, strip_left, strip_right)
    count = lax.axis_size("gy")
    from_low = lax.ppermute(to_up, "gy", [(i, i + 1) for i in range(count - 1)])
    from_high = lax.ppermute(to_down, "gy", [(i + 1, i) for i in range(count - 1)])
    tall = (2 * ROWS, LANES)
    return pl.pallas_call(
        steps_kernel,
        out_shape=(
            jax.ShapeDtypeStruct(flow_moments.shape, f32),
            jax.ShapeDtypeStruct(species_moments.shape, f32),
            jax.ShapeDtypeStruct(fluid_mask.shape, f32),
        ),
        in_specs=vmem(8),
        out_specs=tuple(vmem(3)),
        scratch_shapes=[
            pltpu.VMEM((FIELDS, 12) + tall, f32),
            pltpu.VMEM((NFLOW + NSPEC, 12) + tall, f32),
            pltpu.VMEM((12,) + tall, f32),
            pltpu.VMEM((2, FIELDS) + tall, f32),
            pltpu.VMEM((NFLOW + NSPEC,) + tall, f32),
            pltpu.VMEM((12, ROWS, LANES), f32),
        ],
        compiler_params=params,
    )(block, left, right, strip, strip_left, strip_right, from_low, from_high)


def solution(mesh):
    return jax.shard_map(
        per_device,
        mesh=mesh,
        in_specs=(
            P(None, "gx", "gy", "gz"),
            P(None, "gx", "gy", "gz"),
            P("gx", "gy", "gz"),
            P("gx", "gy", "gz"),
        ),
        out_specs=(P(None, "gx", "gy", "gz"), P(None, "gx", "gy", "gz"), P("gx", "gy", "gz")),
        check_vma=False,
    )
```

```python
import jax
import jax.numpy as jnp
from jax import lax
from jax.experimental import pallas as pl
from jax.experimental.pallas import tpu as pltpu
from jax.sharding import PartitionSpec as P

STEPS = 4
DEEP = 4
KEEP_FLOW = 1.0 - 1.0 / 0.8
KEEP_SPECIES = 1.0 - 1.0 / 0.7
REACT_RATE = 0.5
GRAVITY = 0.001
MOVING = [
    (1, 0, 0),
    (-1, 0, 0),
    (0, 1, 0),
    (0, -1, 0),
    (0, 0, 1),
    (0, 0, -1),
    (1, 1, 0),
    (-1, -1, 0),
    (1, -1, 0),
    (-1, 1, 0),
    (1, 0, 1),
    (-1, 0, -1),
    (1, 0, -1),
    (-1, 0, 1),
    (0, 1, 1),
    (0, -1, -1),
    (0, 1, -1),
    (0, -1, 1),
]
NFLOW = 18
NSPEC = 6
SPECIES_WEIGHT = 0.125
FIELDS = 15
FLUID = 14
NEAR = 3 * FIELDS
HALF = 45 + 7
FAR_ROWS = 5 * FIELDS
ROW_TILES = FAR_ROWS + 7
ROWS = 8
LANES = 128
SOLID = float("nan")
REACTIVE = float("inf")
LARGEST = 3.0e38


def opposite(index):
    return index ^ 1


def flow_populations(m):
    third = m[0] * (1.0 / 3.0)
    axx, ayy, azz = m[4] - third, m[5] - third, m[6] - third
    base = m[0] - 1.5 * (axx + ayy + azz)
    sides = (4.5 * axx, 4.5 * ayy, 4.5 * azz)
    drift = [m[1 + k] * (1.0 / 12.0) for k in range(3)]
    moving = []
    lifted = [base + side for side in sides]
    for k in range(3):
        even, odd = lifted[k] * (1.0 / 18.0), m[1 + k] * (1.0 / 6.0)
        moving += [even + odd, even - odd]
    for a, b, cross in ((0, 1, 7), (0, 2, 8), (1, 2, 9)):
        both = (lifted[a] + sides[b]) * (1.0 / 36.0)
        mixed = m[cross] * 0.25
        same, differ = both + mixed, both - mixed
        plus, minus = drift[a] + drift[b], drift[a] - drift[b]
        moving += [same + plus, same - plus, differ + minus, differ - minus]
    return base * (1.0 / 3.0), moving


def species_populations(s):
    part = s[0] * SPECIES_WEIGHT
    moving = []
    for k in range(3):
        odd = s[1 + k] * 0.5
        moving += [part + odd, part - odd]
    return s[0] * 0.25, moving


def collide(flow, species):
    rho = flow[0]
    j = flow[1:4]
    third = rho * (1.0 / 3.0)
    equil = [third + j[0] * j[0], third + j[1] * j[1], third + j[2] * j[2], j[0] * j[1], j[0] * j[2], j[1] * j[2]]
    stress = [KEEP_FLOW * flow[4 + k] + (1.0 - KEEP_FLOW) * equil[k] for k in range(6)]
    conc = species[0]
    flux = [KEEP_SPECIES * species[1 + k] + (1.0 - KEEP_SPECIES) * (conc * j[k]) for k in range(3)]
    return [rho] + list(j) + stress + [conc] + flux


def is_number(value):
    return value < LARGEST


def pass_on(post, arriving, arriving_species):
    rest, own = flow_populations(post[:10])
    f = []
    for c in range(NFLOW):
        value = arriving[c]
        f.append(jnp.where(is_number(value), value, own[opposite(c)]))
    total = [f[2 * k] + f[2 * k + 1] for k in range(9)]
    diff = [f[2 * k] - f[2 * k + 1] for k in range(9)]
    xy, xz, yz = total[3] + total[4], total[5] + total[6], total[7] + total[8]
    rho = rest + (total[0] + total[1] + total[2]) + (xy + xz + yz)
    jx = diff[0] + (diff[3] + diff[4]) + (diff[5] + diff[6]) + GRAVITY
    jy = diff[1] + (diff[3] - diff[4]) + (diff[7] + diff[8])
    jz = diff[2] + (diff[5] - diff[6]) + (diff[7] - diff[8])
    flow = [
        rho,
        jx,
        jy,
        jz,
        total[0] + xy + xz,
        total[1] + xy + yz,
        total[2] + xz + yz,
        total[3] - total[4],
        total[5] - total[6],
        total[7] - total[8],
    ]
    rest, own = species_populations(post[10:14])
    g = []
    for c in range(NSPEC):
        value = arriving_species[c]
        back = own[opposite(c)]
        slow = jnp.where(value > LARGEST, REACT_RATE, 0.0)
        g.append(jnp.where(is_number(value), value, back + slow * (SPECIES_WEIGHT - back)))
    conc = rest + (g[0] + g[1]) + (g[2] + g[3]) + (g[4] + g[5])
    return flow, [conc, g[0] - g[1], g[2] - g[3], g[4] - g[5]]


def next_post(post, flow, species):
    fluid = is_number(post[0])
    new = collide(flow, species)
    new[0] = jnp.where(fluid, new[0], post[0])
    new[10] = jnp.where(fluid, new[10], post[10])
    for k in range(11, 14):
        new[k] = jnp.where(fluid, new[k], 0.0)
    return new


def lanes_of(shape):
    return lax.broadcasted_iota(jnp.int32, shape, len(shape) - 1)


def rows_of(shape):
    return lax.broadcasted_iota(jnp.int32, shape, len(shape) - 2)


def roll(value, shift, axis):
    size = value.shape[axis]
    if isinstance(shift, int):
        shift = shift % size
        if shift == 0:
            return value
    return pltpu.roll(value, shift, axis)


def first_slot():
    return 4 * lax.rem(lax.axis_index("gx"), 4)


def towards(sign):
    return [c for c in range(NFLOW) if MOVING[c][0] == sign]


def start_kernel(flow_in, species_in, fluid_in, react_in, block_ref, right_ref, left_ref, flow_ref, species_ref, fluid_ref, react_ref, done):
    pairs = ((flow_in, flow_ref), (species_in, species_ref), (fluid_in, fluid_ref), (react_in, react_ref))
    copies = [pltpu.make_async_copy(one, two, done.at[k]) for k, (one, two) in enumerate(pairs)]
    for copy in copies:
        copy.start()
    for copy in copies:
        copy.wait()
    for x in range(DEEP):
        slot = first_slot() + x
        fluid = fluid_ref[x].astype(jnp.float32)
        react = react_ref[x].astype(jnp.float32)
        flow = [flow_ref[k, x] * fluid for k in range(10)]
        species = [species_ref[k, x] * fluid for k in range(4)]
        post = collide(flow, species)
        for far, sign, ref in ((0, 1, right_ref), (3, -1, left_ref)):
            if x == far:
                _, flow_pops = flow_populations(post[:10])
                _, species_pops = species_populations(post[10:])
                parts = [flow_pops[c] for c in towards(sign)] + [species_pops[towards(sign)[0]], fluid]
                parts[0] = jnp.where(fluid > 0.5, parts[0], react)
                for k, value in enumerate(parts):
                    ref[NEAR + k] = roll(value, 8 * slot + 4, 1)
        post[0] = jnp.where(fluid > 0.5, post[0], react)
        for k, value in enumerate(post + [fluid]):
            value = roll(value, 8 * slot + 4, 1)
            block_ref[k, x] = value
            if x > 0:
                right_ref[3 * k + x - 1] = value
            if x < 3:
                left_ref[3 * k + x] = value


def bring_kernel(block_in, block_ref, done):
    copy = pltpu.make_async_copy(block_in, block_ref, done)
    copy.start()
    copy.wait()


def put_rows(up_ref, down_ref, place, one, two):
    high = rows_of((ROWS, LANES)) >= 4
    two = roll(two, 4, 0)
    up_ref[place] = jnp.where(high, one, two)
    down_ref[place] = jnp.where(high, two, one)


def layer_of(field, x, own_ref, left_ref, right_ref):
    if x < 4:
        return left_ref[3 * field + x - 1]
    if x < 8:
        return own_ref[field, x - 4]
    return right_ref[3 * field + x - 8]


def rows_kernel(own_ref, left_ref, right_ref, up_ref, down_ref):
    refs = (own_ref, left_ref, right_ref)
    for field in range(FIELDS):
        for k in range(5):
            put_rows(up_ref, down_ref, 5 * field + k, layer_of(field, k + 1, *refs), layer_of(field, k + 6, *refs))
    for k in range(7):
        put_rows(up_ref, down_ref, FAR_ROWS + k, left_ref[NEAR + k], right_ref[NEAR + k])


def slot_at(x):
    return lax.rem(first_slot() + x + 12, 16)


TALL = (2 * ROWS, LANES)


def halves(up_ref, down_ref, place):
    low = rows_of((ROWS, LANES)) < 4
    up, down = up_ref[place], down_ref[place]
    return jnp.where(low, down, up), roll(jnp.where(low, up, down), 4, 0)


def edges_kernel(own_ref, left_ref, right_ref, up_ref, down_ref, edge_ref):
    refs = (own_ref, left_ref, right_ref)
    slot_of = lanes_of((ROWS, LANES)) // 8
    here = [slot_of == slot_at(x) for x in range(12)]
    for field in range(FIELDS):
        near = jnp.zeros((ROWS, LANES), jnp.float32)
        beyond = near
        for k in range(5):
            one, two = halves(up_ref, down_ref, 5 * field + k)
            for x, value in ((k + 1, one), (k + 6, two)):
                near = jnp.where(here[x], layer_of(field, x, *refs), near)
                beyond = jnp.where(here[x], value, beyond)
        if field < 7:
            one, two = halves(up_ref, down_ref, FAR_ROWS + field)
            for x, value, ref in ((0, one, left_ref), (11, two, right_ref)):
                near = jnp.where(here[x], ref[NEAR + field], near)
                beyond = jnp.where(here[x], value, beyond)
        edge_ref[field, 0:ROWS] = near
        edge_ref[field, ROWS : 2 * ROWS] = beyond


def marked(first, conc, fluid):
    solid = fluid < 0.5
    mark = jnp.where(first > 0.5, REACTIVE, SOLID)
    return jnp.where(solid, SOLID, first), jnp.where(solid, mark, conc)


def marked_far(parts):
    solid = parts[6] < 0.5
    mark = jnp.where(parts[0] > 0.5, REACTIVE, SOLID)
    return [jnp.where(solid, SOLID, part) for part in parts[:5]] + [jnp.where(solid, mark, parts[5])]


def moved(value, c):
    cx, cy, cz = MOVING[c]
    return roll(roll(value, 8 * cx + cz, 1), cy, 0)


def send(state_ref, sent_ref, x):
    _, flow_pops = flow_populations([state_ref[k, x] for k in range(10)])
    _, species_pops = species_populations([state_ref[k, x] for k in range(10, 14)])
    for c in range(NFLOW):
        sent_ref[c, x] = moved(flow_pops[c], c)
    for c in range(NSPEC):
        sent_ref[NFLOW + c, x] = moved(species_pops[c], c)


def first_sends_kernel(own_ref, left_ref, right_ref, up_ref, down_ref, state_ref, sent_ref):
    refs = (own_ref, left_ref, right_ref)
    for field in (FLUID,) + tuple(range(FLUID)):
        for k in range(5):
            one, two = halves(up_ref, down_ref, 5 * field + k)
            for x, value in ((k + 1, one), (k + 6, two)):
                state_ref[field, x, 0:ROWS] = layer_of(field, x, *refs)
                state_ref[field, x, ROWS : 2 * ROWS] = value
    for x in range(1, 11):
        rho, conc = marked(state_ref[0, x], state_ref[10, x], state_ref[FLUID, x])
        state_ref[0, x] = rho
        state_ref[10, x] = conc
        send(state_ref, sent_ref, x)
    beyond = [halves(up_ref, down_ref, FAR_ROWS + k) for k in range(7)]
    for end, (x, sign, ref) in enumerate(((0, 1, left_ref), (11, -1, right_ref))):
        parts = [jnp.concatenate([ref[NEAR + k], beyond[k][end]]) for k in range(7)]
        parts = marked_far(parts)
        along = towards(sign)
        for k, c in enumerate(along):
            sent_ref[c, x] = moved(parts[k], c)
        sent_ref[NFLOW + along[0], x] = moved(parts[5], along[0])


def steps_kernel(
    first_state,
    first_sent,
    edge_ref,
    below_ref,
    above_ref,
    flow_out,
    species_out,
    dissolved_out,
    state,
    sent,
    strips,
    strip_sent,
):
    lane = lanes_of(TALL)
    inner = lane % 8 < 4

    far_strips = []
    for side in range(2):
        for field in range(FIELDS):
            near, beyond = edge_ref[field], (below_ref, above_ref)[side][field]
            strips[side, field] = jnp.where(inner, near, beyond) if side else jnp.where(inner, beyond, near)
        far_strips.append(marked_far([strips[side, k] for k in range(7)]))
        rho, conc = marked(strips[side, 0], strips[side, 10], strips[side, FLUID])
        strips[side, 0] = rho
        strips[side, 10] = conc

    def turned_back(value, x):
        return roll(value, 124 - 8 * slot_at(x), 1)

    released = [jnp.zeros((ROWS, LANES), jnp.float32)] * DEEP
    for step in range(STEPS):
        last = step == STEPS - 1
        state_now, sent_now = (first_state, first_sent) if step == 0 else (state, sent)
        for side in range(2):
            post = [strips[side, k] for k in range(14)]
            _, flow_pops = flow_populations(post[:10])
            _, species_pops = species_populations(post[10:])
            if step == 0:
                for x, sign in ((0, 1), (11, -1)):
                    here = lane // 8 == slot_at(x)
                    for k, c in enumerate(towards(sign)):
                        flow_pops[c] = jnp.where(here, far_strips[side][k], flow_pops[c])
                    c = towards(sign)[0]
                    species_pops[c] = jnp.where(here, far_strips[side][5], species_pops[c])
            wanted = [c for c in range(NFLOW) if not last or MOVING[c][2] == (1, -1)[side]]
            arriving = {c: moved(flow_pops[c], c) for c in wanted}
            arriving_species = {c: moved(species_pops[c], c) for c in wanted if c < NSPEC}
            for c in wanted:
                if MOVING[c][2] == (1, -1)[side]:
                    strip_sent[c] = arriving[c]
                    if c < NSPEC:
                        strip_sent[NFLOW + c] = arriving_species[c]
            if not last:
                new_flow, new_species = pass_on(post, arriving, arriving_species)
                for k, value in enumerate(next_post(post, new_flow, new_species)):
                    strips[side, k] = value
        if step > 0:
            for x in range(step, 12 - step):
                send(state, sent, x)
        height = ROWS if last else 2 * ROWS
        for x in range(step + 1, 11 - step):
            first = lane[0:height] == 8 * slot_at(x) + 4
            end = lane[0:height] == 8 * slot_at(x) + 3

            def arrives(place, c):
                cx, _, cz = MOVING[c]
                value = sent_now[place, x - cx, 0:height]
                if cz:
                    value = jnp.where(first if cz > 0 else end, strip_sent[place, 0:height], value)
                return value

            post = [state_now[k, x, 0:height] for k in range(14)]
            arriving = [arrives(c, c) for c in range(NFLOW)]
            arriving_species = [arrives(NFLOW + c, c) for c in range(NSPEC)]
            new_flow, new_species = pass_on(post, arriving, arriving_species)
            if 0 <= x - DEEP < DEEP:
                parts = [value[0:ROWS] for value in arriving_species]
                parts = [jnp.where(is_number(part), SPECIES_WEIGHT - part, 0.0) for part in parts]
                parts = (parts[0] + parts[1]) + (parts[2] + parts[3]) + (parts[4] + parts[5])
                released[x - DEEP] = released[x - DEEP] + parts
            if last:
                fluid = is_number(post[0])
                for k in range(10):
                    flow_out[k, x - DEEP] = turned_back(jnp.where(fluid, new_flow[k], 0.0), x)
                for k in range(4):
                    species_out[k, x - DEEP] = turned_back(jnp.where(fluid, new_species[k], 0.0), x)
                gone = jnp.where(post[10] > LARGEST, REACT_RATE * released[x - DEEP], 0.0)
                dissolved_out[x - DEEP] = turned_back(gone, x)
            else:
                for k, value in enumerate(next_post(post, new_flow, new_species)):
                    state[k, x] = value


def shifted(upward, downward, axis, wrap):
    count = lax.axis_size(axis)
    up = [(i, (i + 1) % count) for i in range(count if wrap else count - 1)]
    down = [(j, i) for i, j in up]
    return lax.ppermute(upward, axis, up), lax.ppermute(downward, axis, down)


def vmem(count):
    return [pl.BlockSpec(memory_space=pltpu.VMEM)] * count


def per_device(flow_moments, species_moments, fluid_mask, reactive_mask):
    f32 = jnp.float32
    small = pltpu.CompilerParams(vmem_limit_bytes=16 * 1024 * 1024)
    half = jax.ShapeDtypeStruct((HALF, ROWS, LANES), f32)
    block, to_right, to_left = pl.pallas_call(
        start_kernel,
        out_shape=(jax.ShapeDtypeStruct((FIELDS, DEEP, ROWS, LANES), f32), half, half),
        in_specs=[pl.BlockSpec(memory_space=pltpu.HBM)] * 4,
        out_specs=tuple(vmem(3)),
        scratch_shapes=[
            pltpu.VMEM(flow_moments.shape, f32),
            pltpu.VMEM(species_moments.shape, f32),
            pltpu.VMEM(fluid_mask.shape, fluid_mask.dtype),
            pltpu.VMEM(reactive_mask.shape, reactive_mask.dtype),
            pltpu.SemaphoreType.DMA((4,)),
        ],
        compiler_params=pltpu.CompilerParams(vmem_limit_bytes=56 * 1024 * 1024),
    )(flow_moments, species_moments, fluid_mask, reactive_mask)
    left, right = shifted(to_right, to_left, "gx", True)
    block = pl.pallas_call(
        bring_kernel,
        out_shape=jax.ShapeDtypeStruct(block.shape, f32),
        in_specs=[pl.BlockSpec(memory_space=pltpu.HBM)],
        out_specs=vmem(1)[0],
        scratch_shapes=[pltpu.SemaphoreType.DMA],
        compiler_params=small,
        cost_estimate=pl.CostEstimate(flops=10**7, bytes_accessed=10**7, transcendentals=0),
    )(block)
    tiles = jax.ShapeDtypeStruct((ROW_TILES, ROWS, LANES), f32)
    to_up, to_down = pl.pallas_call(
        rows_kernel,
        out_shape=(tiles, tiles),
        in_specs=vmem(3),
        out_specs=tuple(vmem(2)),
        compiler_params=small,
    )(block, left, right)
    from_low, from_high = shifted(to_up, to_down, "gy", False)
    strips = jax.ShapeDtypeStruct((FIELDS,) + TALL, f32)
    edge = pl.pallas_call(
        edges_kernel,
        out_shape=strips,
        in_specs=vmem(5),
        out_specs=vmem(1)[0],
        compiler_params=small,
    )(block, left, right, from_low, from_high)
    below, above = shifted(edge, edge, "gz", False)
    state, sent = pl.pallas_call(
        first_sends_kernel,
        out_shape=(
            jax.ShapeDtypeStruct((FIELDS, 12) + TALL, f32),
            jax.ShapeDtypeStruct((NFLOW + NSPEC, 12) + TALL, f32),
        ),
        in_specs=vmem(5),
        out_specs=tuple(vmem(2)),
        compiler_params=small,
        cost_estimate=pl.CostEstimate(flops=10**7, bytes_accessed=10**7, transcendentals=0),
    )(block, left, right, from_low, from_high)
    return pl.pallas_call(
        steps_kernel,
        out_shape=(
            jax.ShapeDtypeStruct(flow_moments.shape, f32),
            jax.ShapeDtypeStruct(species_moments.shape, f32),
            jax.ShapeDtypeStruct(fluid_mask.shape, f32),
        ),
        in_specs=vmem(5),
        out_specs=tuple(vmem(3)),
        scratch_shapes=[
            pltpu.VMEM((FIELDS, 12) + TALL, f32),
            pltpu.VMEM((NFLOW + NSPEC, 12) + TALL, f32),
            pltpu.VMEM((2, FIELDS) + TALL, f32),
            pltpu.VMEM((NFLOW + NSPEC,) + TALL, f32),
        ],
        compiler_params=small,
    )(state, sent, edge, below, above)


def solution(mesh):
    return jax.shard_map(
        per_device,
        mesh=mesh,
        in_specs=(
            P(None, "gx", "gy", "gz"),
            P(None, "gx", "gy", "gz"),
            P("gx", "gy", "gz"),
            P("gx", "gy", "gz"),
        ),
        out_specs=(P(None, "gx", "gy", "gz"), P(None, "gx", "gy", "gz"), P("gx", "gy", "gz")),
        check_vma=False,
    )
```

```python
import jax
import jax.numpy as jnp
from jax import lax
from jax.experimental import pallas as pl
from jax.experimental.pallas import tpu as pltpu
from jax.sharding import PartitionSpec as P

STEPS = 4
DEEP = 4
KEEP_FLOW = 1.0 - 1.0 / 0.8
KEEP_SPECIES = 1.0 - 1.0 / 0.7
REACT_RATE = 0.5
GRAVITY = 0.001
MOVING = [
    (1, 0, 0),
    (-1, 0, 0),
    (0, 1, 0),
    (0, -1, 0),
    (0, 0, 1),
    (0, 0, -1),
    (1, 1, 0),
    (-1, -1, 0),
    (1, -1, 0),
    (-1, 1, 0),
    (1, 0, 1),
    (-1, 0, -1),
    (1, 0, -1),
    (-1, 0, 1),
    (0, 1, 1),
    (0, -1, -1),
    (0, 1, -1),
    (0, -1, 1),
]
NFLOW = 18
NSPEC = 6
SPECIES_WEIGHT = 0.125
FIELDS = 15
FLUID = 14
NEAR = 3 * FIELDS
HALF = 45 + 7
OWN_TILES = 2 * FIELDS
FAR_ROWS = 3 * FIELDS
ROWS = 8
LANES = 128
SOLID = float("nan")
REACTIVE = float("inf")
LARGEST = 3.0e38


def opposite(index):
    return index ^ 1


def flow_populations(m):
    third = m[0] * (1.0 / 3.0)
    axx, ayy, azz = m[4] - third, m[5] - third, m[6] - third
    base = m[0] - 1.5 * (axx + ayy + azz)
    sides = (4.5 * axx, 4.5 * ayy, 4.5 * azz)
    drift = [m[1 + k] * (1.0 / 12.0) for k in range(3)]
    moving = []
    lifted = [base + side for side in sides]
    for k in range(3):
        even, odd = lifted[k] * (1.0 / 18.0), m[1 + k] * (1.0 / 6.0)
        moving += [even + odd, even - odd]
    for a, b, cross in ((0, 1, 7), (0, 2, 8), (1, 2, 9)):
        both = (lifted[a] + sides[b]) * (1.0 / 36.0)
        mixed = m[cross] * 0.25
        same, differ = both + mixed, both - mixed
        plus, minus = drift[a] + drift[b], drift[a] - drift[b]
        moving += [same + plus, same - plus, differ + minus, differ - minus]
    return base * (1.0 / 3.0), moving


def species_populations(s):
    part = s[0] * SPECIES_WEIGHT
    moving = []
    for k in range(3):
        odd = s[1 + k] * 0.5
        moving += [part + odd, part - odd]
    return s[0] * 0.25, moving


def collide(flow, species):
    rho = flow[0]
    j = flow[1:4]
    third = rho * (1.0 / 3.0)
    equil = [third + j[0] * j[0], third + j[1] * j[1], third + j[2] * j[2], j[0] * j[1], j[0] * j[2], j[1] * j[2]]
    stress = [KEEP_FLOW * flow[4 + k] + (1.0 - KEEP_FLOW) * equil[k] for k in range(6)]
    conc = species[0]
    flux = [KEEP_SPECIES * species[1 + k] + (1.0 - KEEP_SPECIES) * (conc * j[k]) for k in range(3)]
    return [rho] + list(j) + stress + [conc] + flux


def is_number(value):
    return value < LARGEST


def pass_on(post, arriving, arriving_species):
    rest, own = flow_populations(post[:10])
    f = []
    for c in range(NFLOW):
        value = arriving[c]
        f.append(jnp.where(is_number(value), value, own[opposite(c)]))
    total = [f[2 * k] + f[2 * k + 1] for k in range(9)]
    diff = [f[2 * k] - f[2 * k + 1] for k in range(9)]
    xy, xz, yz = total[3] + total[4], total[5] + total[6], total[7] + total[8]
    rho = rest + (total[0] + total[1] + total[2]) + (xy + xz + yz)
    jx = diff[0] + (diff[3] + diff[4]) + (diff[5] + diff[6]) + GRAVITY
    jy = diff[1] + (diff[3] - diff[4]) + (diff[7] + diff[8])
    jz = diff[2] + (diff[5] - diff[6]) + (diff[7] - diff[8])
    flow = [
        rho,
        jx,
        jy,
        jz,
        total[0] + xy + xz,
        total[1] + xy + yz,
        total[2] + xz + yz,
        total[3] - total[4],
        total[5] - total[6],
        total[7] - total[8],
    ]
    rest, own = species_populations(post[10:14])
    g = []
    for c in range(NSPEC):
        value = arriving_species[c]
        back = own[opposite(c)]
        slow = jnp.where(value > LARGEST, REACT_RATE, 0.0)
        g.append(jnp.where(is_number(value), value, back + slow * (SPECIES_WEIGHT - back)))
    conc = rest + (g[0] + g[1]) + (g[2] + g[3]) + (g[4] + g[5])
    return flow, [conc, g[0] - g[1], g[2] - g[3], g[4] - g[5]]


def next_post(post, flow, species):
    fluid = is_number(post[0])
    new = collide(flow, species)
    new[0] = jnp.where(fluid, new[0], post[0])
    new[10] = jnp.where(fluid, new[10], post[10])
    for k in range(11, 14):
        new[k] = jnp.where(fluid, new[k], 0.0)
    return new


def lanes_of(shape):
    return lax.broadcasted_iota(jnp.int32, shape, len(shape) - 1)


def rows_of(shape):
    return lax.broadcasted_iota(jnp.int32, shape, len(shape) - 2)


def roll(value, shift, axis):
    size = value.shape[axis]
    if isinstance(shift, int):
        shift = shift % size
        if shift == 0:
            return value
    return pltpu.roll(value, shift, axis)


def first_slot():
    return 4 * lax.rem(lax.axis_index("gx"), 4)


def towards(sign):
    return [c for c in range(NFLOW) if MOVING[c][0] == sign]


def start_kernel(flow_in, species_in, fluid_in, react_in, block_ref, right_ref, left_ref, flow_ref, species_ref, fluid_ref, react_ref, done):
    pairs = ((flow_in, flow_ref), (species_in, species_ref), (fluid_in, fluid_ref), (react_in, react_ref))
    copies = [pltpu.make_async_copy(one, two, done.at[k]) for k, (one, two) in enumerate(pairs)]
    for copy in copies:
        copy.start()
    for copy in copies:
        copy.wait()
    for x in range(DEEP):
        slot = first_slot() + x
        fluid = fluid_ref[x].astype(jnp.float32)
        react = react_ref[x].astype(jnp.float32)
        flow = [flow_ref[k, x] * fluid for k in range(10)]
        species = [species_ref[k, x] * fluid for k in range(4)]
        post = collide(flow, species)
        for far, sign, ref in ((0, 1, right_ref), (3, -1, left_ref)):
            if x == far:
                _, flow_pops = flow_populations(post[:10])
                _, species_pops = species_populations(post[10:])
                parts = [flow_pops[c] for c in towards(sign)] + [species_pops[towards(sign)[0]], fluid]
                parts[0] = jnp.where(fluid > 0.5, parts[0], react)
                for k, value in enumerate(parts):
                    ref[NEAR + k] = roll(value, 8 * slot + 4, 1)
        post[0] = jnp.where(fluid > 0.5, post[0], react)
        for k, value in enumerate(post + [fluid]):
            value = roll(value, 8 * slot + 4, 1)
            block_ref[k, x] = value
            if x > 0:
                right_ref[3 * k + x - 1] = value
            if x < 3:
                left_ref[3 * k + x] = value


def put_rows(up_ref, down_ref, place, one, two):
    high = rows_of((ROWS, LANES)) >= 4
    two = roll(two, 4, 0)
    up_ref[place] = jnp.where(high, one, two)
    down_ref[place] = jnp.where(high, two, one)


def layer_of(field, x, own_ref, left_ref, right_ref):
    if x < 4:
        return left_ref[3 * field + x - 1]
    if x < 8:
        return own_ref[field, x - 4]
    return right_ref[3 * field + x - 8]


def own_rows_kernel(block_in, block_ref, up_ref, down_ref, done):
    copy = pltpu.make_async_copy(block_in, block_ref, done)
    copy.start()
    copy.wait()
    for field in range(FIELDS):
        for k in range(2):
            put_rows(up_ref, down_ref, 2 * field + k, block_ref[field, k], block_ref[field, k + 2])


def rows_kernel(left_ref, right_ref, own_up, own_down, up_ref, down_ref):
    for k in range(HALF):
        put_rows(up_ref, down_ref, k, left_ref[k], right_ref[k])


def slot_at(x):
    return lax.rem(first_slot() + x + 12, 16)


TALL = (2 * ROWS, LANES)


def halves(up_ref, down_ref, place):
    low = rows_of((ROWS, LANES)) < 4
    up, down = up_ref[place], down_ref[place]
    return jnp.where(low, down, up), roll(jnp.where(low, up, down), 4, 0)


def layer_of(field, x, own_ref, left_ref, right_ref):
    if x < 4:
        return left_ref[3 * field + x - 1]
    if x < 8:
        return own_ref[field, x - 4]
    return right_ref[3 * field + x - 8]


def rows_beyond(field, own_up, own_down, up_ref, down_ref):
    found = {}
    for k in range(2):
        found[4 + k], found[6 + k] = halves(own_up, own_down, 2 * field + k)
    for k in range(3):
        found[1 + k], found[8 + k] = halves(up_ref, down_ref, 3 * field + k)
    return found


def edges_kernel(own_ref, left_ref, right_ref, own_up, own_down, up_ref, down_ref, edge_ref):
    refs = (own_ref, left_ref, right_ref)
    slot_of = lanes_of((ROWS, LANES)) // 8
    here = [slot_of == slot_at(x) for x in range(12)]
    for field in range(FIELDS):
        near = jnp.zeros((ROWS, LANES), jnp.float32)
        beyond = near
        for x, value in rows_beyond(field, own_up, own_down, up_ref, down_ref).items():
            near = jnp.where(here[x], layer_of(field, x, *refs), near)
            beyond = jnp.where(here[x], value, beyond)
        if field < 7:
            one, two = halves(up_ref, down_ref, FAR_ROWS + field)
            for x, value, ref in ((0, one, left_ref), (11, two, right_ref)):
                near = jnp.where(here[x], ref[NEAR + field], near)
                beyond = jnp.where(here[x], value, beyond)
        edge_ref[field, 0:ROWS] = near
        edge_ref[field, ROWS : 2 * ROWS] = beyond


def marked(first, conc, fluid):
    solid = fluid < 0.5
    mark = jnp.where(first > 0.5, REACTIVE, SOLID)
    return jnp.where(solid, SOLID, first), jnp.where(solid, mark, conc)


def marked_far(parts):
    solid = parts[6] < 0.5
    mark = jnp.where(parts[0] > 0.5, REACTIVE, SOLID)
    return [jnp.where(solid, SOLID, part) for part in parts[:5]] + [jnp.where(solid, mark, parts[5])]


def moved(value, c):
    cx, cy, cz = MOVING[c]
    return roll(roll(value, 8 * cx + cz, 1), cy, 0)


def send(state_ref, sent_ref, x):
    _, flow_pops = flow_populations([state_ref[k, x] for k in range(10)])
    _, species_pops = species_populations([state_ref[k, x] for k in range(10, 14)])
    for c in range(NFLOW):
        sent_ref[c, x] = moved(flow_pops[c], c)
    for c in range(NSPEC):
        sent_ref[NFLOW + c, x] = moved(species_pops[c], c)


def first_sends_kernel(own_ref, left_ref, right_ref, own_up, own_down, up_ref, down_ref, state_ref, sent_ref):
    refs = (own_ref, left_ref, right_ref)
    for field in range(FIELDS):
        for x, value in rows_beyond(field, own_up, own_down, up_ref, down_ref).items():
            state_ref[field, x, 0:ROWS] = layer_of(field, x, *refs)
            state_ref[field, x, ROWS : 2 * ROWS] = value
    for x in range(1, 11):
        rho, conc = marked(state_ref[0, x], state_ref[10, x], state_ref[FLUID, x])
        state_ref[0, x] = rho
        state_ref[10, x] = conc
        send(state_ref, sent_ref, x)
    beyond = [halves(up_ref, down_ref, FAR_ROWS + k) for k in range(7)]
    for end, (x, sign, ref) in enumerate(((0, 1, left_ref), (11, -1, right_ref))):
        parts = [jnp.concatenate([ref[NEAR + k], beyond[k][end]]) for k in range(7)]
        parts = marked_far(parts)
        along = towards(sign)
        for k, c in enumerate(along):
            sent_ref[c, x] = moved(parts[k], c)
        sent_ref[NFLOW + along[0], x] = moved(parts[5], along[0])


def steps_kernel(
    first_state,
    first_sent,
    edge_ref,
    below_ref,
    above_ref,
    flow_out,
    species_out,
    dissolved_out,
    state,
    sent,
    strips,
    strip_sent,
):
    lane = lanes_of(TALL)
    inner = lane % 8 < 4

    far_strips = []
    for side in range(2):
        for field in range(FIELDS):
            near, beyond = edge_ref[field], (below_ref, above_ref)[side][field]
            strips[side, field] = jnp.where(inner, near, beyond) if side else jnp.where(inner, beyond, near)
        far_strips.append(marked_far([strips[side, k] for k in range(7)]))
        rho, conc = marked(strips[side, 0], strips[side, 10], strips[side, FLUID])
        strips[side, 0] = rho
        strips[side, 10] = conc

    def turned_back(value, x):
        return roll(value, 124 - 8 * slot_at(x), 1)

    released = [jnp.zeros((ROWS, LANES), jnp.float32)] * DEEP
    for step in range(STEPS):
        last = step == STEPS - 1
        state_now, sent_now = (first_state, first_sent) if step == 0 else (state, sent)
        for side in range(2):
            post = [strips[side, k] for k in range(14)]
            _, flow_pops = flow_populations(post[:10])
            _, species_pops = species_populations(post[10:])
            if step == 0:
                for x, sign in ((0, 1), (11, -1)):
                    here = lane // 8 == slot_at(x)
                    for k, c in enumerate(towards(sign)):
                        flow_pops[c] = jnp.where(here, far_strips[side][k], flow_pops[c])
                    c = towards(sign)[0]
                    species_pops[c] = jnp.where(here, far_strips[side][5], species_pops[c])
            wanted = [c for c in range(NFLOW) if not last or MOVING[c][2] == (1, -1)[side]]
            arriving = {c: moved(flow_pops[c], c) for c in wanted}
            arriving_species = {c: moved(species_pops[c], c) for c in wanted if c < NSPEC}
            for c in wanted:
                if MOVING[c][2] == (1, -1)[side]:
                    strip_sent[c] = arriving[c]
                    if c < NSPEC:
                        strip_sent[NFLOW + c] = arriving_species[c]
            if not last:
                new_flow, new_species = pass_on(post, arriving, arriving_species)
                for k, value in enumerate(next_post(post, new_flow, new_species)):
                    strips[side, k] = value
        if step > 0:
            for x in range(step, 12 - step):
                send(state, sent, x)
        height = ROWS if last else 2 * ROWS
        for x in range(step + 1, 11 - step):
            first = lane[0:height] == 8 * slot_at(x) + 4
            end = lane[0:height] == 8 * slot_at(x) + 3

            def arrives(place, c):
                cx, _, cz = MOVING[c]
                value = sent_now[place, x - cx, 0:height]
                if cz:
                    value = jnp.where(first if cz > 0 else end, strip_sent[place, 0:height], value)
                return value

            post = [state_now[k, x, 0:height] for k in range(14)]
            arriving = [arrives(c, c) for c in range(NFLOW)]
            arriving_species = [arrives(NFLOW + c, c) for c in range(NSPEC)]
            new_flow, new_species = pass_on(post, arriving, arriving_species)
            if 0 <= x - DEEP < DEEP:
                parts = [value[0:ROWS] for value in arriving_species]
                parts = [jnp.where(is_number(part), SPECIES_WEIGHT - part, 0.0) for part in parts]
                parts = (parts[0] + parts[1]) + (parts[2] + parts[3]) + (parts[4] + parts[5])
                released[x - DEEP] = released[x - DEEP] + parts
            if last:
                fluid = is_number(post[0])
                for k in range(10):
                    flow_out[k, x - DEEP] = turned_back(jnp.where(fluid, new_flow[k], 0.0), x)
                for k in range(4):
                    species_out[k, x - DEEP] = turned_back(jnp.where(fluid, new_species[k], 0.0), x)
                gone = jnp.where(post[10] > LARGEST, REACT_RATE * released[x - DEEP], 0.0)
                dissolved_out[x - DEEP] = turned_back(gone, x)
            else:
                for k, value in enumerate(next_post(post, new_flow, new_species)):
                    state[k, x] = value


def shifted(upward, downward, axis, wrap):
    count = lax.axis_size(axis)
    up = [(i, (i + 1) % count) for i in range(count if wrap else count - 1)]
    down = [(j, i) for i, j in up]
    return lax.ppermute(upward, axis, up), lax.ppermute(downward, axis, down)


def vmem(count):
    return [pl.BlockSpec(memory_space=pltpu.VMEM)] * count


def per_device(flow_moments, species_moments, fluid_mask, reactive_mask):
    f32 = jnp.float32
    small = pltpu.CompilerParams(vmem_limit_bytes=16 * 1024 * 1024)
    half = jax.ShapeDtypeStruct((HALF, ROWS, LANES), f32)
    block, to_right, to_left = pl.pallas_call(
        start_kernel,
        out_shape=(jax.ShapeDtypeStruct((FIELDS, DEEP, ROWS, LANES), f32), half, half),
        in_specs=[pl.BlockSpec(memory_space=pltpu.HBM)] * 4,
        out_specs=tuple(vmem(3)),
        scratch_shapes=[
            pltpu.VMEM(flow_moments.shape, f32),
            pltpu.VMEM(species_moments.shape, f32),
            pltpu.VMEM(fluid_mask.shape, fluid_mask.dtype),
            pltpu.VMEM(reactive_mask.shape, reactive_mask.dtype),
            pltpu.SemaphoreType.DMA((4,)),
        ],
        compiler_params=pltpu.CompilerParams(vmem_limit_bytes=56 * 1024 * 1024),
    )(flow_moments, species_moments, fluid_mask, reactive_mask)
    left, right = shifted(to_right, to_left, "gx", True)
    own_tiles = jax.ShapeDtypeStruct((OWN_TILES, ROWS, LANES), f32)
    block, own_to_up, own_to_down = pl.pallas_call(
        own_rows_kernel,
        out_shape=(jax.ShapeDtypeStruct(block.shape, f32), own_tiles, own_tiles),
        in_specs=[pl.BlockSpec(memory_space=pltpu.HBM)],
        out_specs=tuple(vmem(3)),
        scratch_shapes=[pltpu.SemaphoreType.DMA],
        compiler_params=small,
        cost_estimate=pl.CostEstimate(flops=10**7, bytes_accessed=10**7, transcendentals=0),
    )(block)
    own_rows = shifted(own_to_up, own_to_down, "gy", False)
    tiles = jax.ShapeDtypeStruct((HALF, ROWS, LANES), f32)
    to_up, to_down = pl.pallas_call(
        rows_kernel,
        out_shape=(tiles, tiles),
        in_specs=vmem(2) + [pl.BlockSpec(memory_space=pl.ANY)] * 2,
        out_specs=tuple(vmem(2)),
        compiler_params=small,
    )(left, right, *own_rows)
    rows = own_rows + shifted(to_up, to_down, "gy", False)
    strips = jax.ShapeDtypeStruct((FIELDS,) + TALL, f32)
    edge = pl.pallas_call(
        edges_kernel,
        out_shape=strips,
        in_specs=vmem(7),
        out_specs=vmem(1)[0],
        compiler_params=small,
    )(block, left, right, *rows)
    below, above = shifted(edge, edge, "gz", False)
    state, sent = pl.pallas_call(
        first_sends_kernel,
        out_shape=(
            jax.ShapeDtypeStruct((FIELDS, 12) + TALL, f32),
            jax.ShapeDtypeStruct((NFLOW + NSPEC, 12) + TALL, f32),
        ),
        in_specs=vmem(7),
        out_specs=tuple(vmem(2)),
        compiler_params=small,
        cost_estimate=pl.CostEstimate(flops=10**7, bytes_accessed=10**7, transcendentals=0),
    )(block, left, right, *rows)
    return pl.pallas_call(
        steps_kernel,
        out_shape=(
            jax.ShapeDtypeStruct(flow_moments.shape, f32),
            jax.ShapeDtypeStruct(species_moments.shape, f32),
            jax.ShapeDtypeStruct(fluid_mask.shape, f32),
        ),
        in_specs=vmem(5),
        out_specs=tuple(vmem(3)),
        scratch_shapes=[
            pltpu.VMEM((FIELDS, 12) + TALL, f32),
            pltpu.VMEM((NFLOW + NSPEC, 12) + TALL, f32),
            pltpu.VMEM((2, FIELDS) + TALL, f32),
            pltpu.VMEM((NFLOW + NSPEC,) + TALL, f32),
        ],
        compiler_params=small,
    )(state, sent, edge, below, above)


def solution(mesh):
    return jax.shard_map(
        per_device,
        mesh=mesh,
        in_specs=(
            P(None, "gx", "gy", "gz"),
            P(None, "gx", "gy", "gz"),
            P("gx", "gy", "gz"),
            P("gx", "gy", "gz"),
        ),
        out_specs=(P(None, "gx", "gy", "gz"), P(None, "gx", "gy", "gz"), P("gx", "gy", "gz")),
        check_vma=False,
    )
```

```python
import jax
import jax.numpy as jnp
from jax import lax
from jax.experimental import pallas as pl
from jax.experimental.pallas import tpu as pltpu
from jax.sharding import PartitionSpec as P

STEPS = 4
DEEP = 4
KEEP_FLOW = 1.0 - 1.0 / 0.8
KEEP_SPECIES = 1.0 - 1.0 / 0.7
REACT_RATE = 0.5
GRAVITY = 0.001
MOVING = [
    (1, 0, 0),
    (-1, 0, 0),
    (0, 1, 0),
    (0, -1, 0),
    (0, 0, 1),
    (0, 0, -1),
    (1, 1, 0),
    (-1, -1, 0),
    (1, -1, 0),
    (-1, 1, 0),
    (1, 0, 1),
    (-1, 0, -1),
    (1, 0, -1),
    (-1, 0, 1),
    (0, 1, 1),
    (0, -1, -1),
    (0, 1, -1),
    (0, -1, 1),
]
NFLOW = 18
NSPEC = 6
SPECIES_WEIGHT = 0.125
FIELDS = 15
FLUID = 14
NEAR = 3 * FIELDS
HALF = 45 + 7
OWN_TILES = 2 * FIELDS
FAR_ROWS = 3 * FIELDS
ROWS = 8
LANES = 128
SOLID = float("nan")
REACTIVE = float("inf")
LARGEST = 3.0e38


def opposite(index):
    return index ^ 1


def flow_populations(m):
    third = m[0] * (1.0 / 3.0)
    axx, ayy, azz = m[4] - third, m[5] - third, m[6] - third
    base = m[0] - 1.5 * (axx + ayy + azz)
    sides = (4.5 * axx, 4.5 * ayy, 4.5 * azz)
    drift = [m[1 + k] * (1.0 / 12.0) for k in range(3)]
    moving = []
    lifted = [base + side for side in sides]
    for k in range(3):
        even, odd = lifted[k] * (1.0 / 18.0), m[1 + k] * (1.0 / 6.0)
        moving += [even + odd, even - odd]
    for a, b, cross in ((0, 1, 7), (0, 2, 8), (1, 2, 9)):
        both = (lifted[a] + sides[b]) * (1.0 / 36.0)
        mixed = m[cross] * 0.25
        same, differ = both + mixed, both - mixed
        plus, minus = drift[a] + drift[b], drift[a] - drift[b]
        moving += [same + plus, same - plus, differ + minus, differ - minus]
    return base * (1.0 / 3.0), moving


def species_populations(s):
    part = s[0] * SPECIES_WEIGHT
    moving = []
    for k in range(3):
        odd = s[1 + k] * 0.5
        moving += [part + odd, part - odd]
    return s[0] * 0.25, moving


def collide(flow, species):
    rho = flow[0]
    j = flow[1:4]
    third = rho * (1.0 / 3.0)
    equil = [third + j[0] * j[0], third + j[1] * j[1], third + j[2] * j[2], j[0] * j[1], j[0] * j[2], j[1] * j[2]]
    stress = [KEEP_FLOW * flow[4 + k] + (1.0 - KEEP_FLOW) * equil[k] for k in range(6)]
    conc = species[0]
    flux = [KEEP_SPECIES * species[1 + k] + (1.0 - KEEP_SPECIES) * (conc * j[k]) for k in range(3)]
    return [rho] + list(j) + stress + [conc] + flux


def is_number(value):
    return value < LARGEST


def pass_on(post, arriving, arriving_species):
    rest, own = flow_populations(post[:10])
    f = []
    for c in range(NFLOW):
        value = arriving[c]
        f.append(jnp.where(is_number(value), value, own[opposite(c)]))
    total = [f[2 * k] + f[2 * k + 1] for k in range(9)]
    diff = [f[2 * k] - f[2 * k + 1] for k in range(9)]
    xy, xz, yz = total[3] + total[4], total[5] + total[6], total[7] + total[8]
    rho = rest + (total[0] + total[1] + total[2]) + (xy + xz + yz)
    jx = diff[0] + (diff[3] + diff[4]) + (diff[5] + diff[6]) + GRAVITY
    jy = diff[1] + (diff[3] - diff[4]) + (diff[7] + diff[8])
    jz = diff[2] + (diff[5] - diff[6]) + (diff[7] - diff[8])
    flow = [
        rho,
        jx,
        jy,
        jz,
        total[0] + xy + xz,
        total[1] + xy + yz,
        total[2] + xz + yz,
        total[3] - total[4],
        total[5] - total[6],
        total[7] - total[8],
    ]
    rest, own = species_populations(post[10:14])
    g = []
    for c in range(NSPEC):
        value = arriving_species[c]
        back = own[opposite(c)]
        slow = jnp.where(value > LARGEST, REACT_RATE, 0.0)
        g.append(jnp.where(is_number(value), value, back + slow * (SPECIES_WEIGHT - back)))
    conc = rest + (g[0] + g[1]) + (g[2] + g[3]) + (g[4] + g[5])
    return flow, [conc, g[0] - g[1], g[2] - g[3], g[4] - g[5]]


def next_post(post, flow, species):
    fluid = is_number(post[0])
    new = collide(flow, species)
    new[0] = jnp.where(fluid, new[0], post[0])
    new[10] = jnp.where(fluid, new[10], post[10])
    for k in range(11, 14):
        new[k] = jnp.where(fluid, new[k], 0.0)
    return new


def lanes_of(shape):
    return lax.broadcasted_iota(jnp.int32, shape, len(shape) - 1)


def rows_of(shape):
    return lax.broadcasted_iota(jnp.int32, shape, len(shape) - 2)


def roll(value, shift, axis):
    size = value.shape[axis]
    if isinstance(shift, int):
        shift = shift % size
        if shift == 0:
            return value
    return pltpu.roll(value, shift, axis)


def base_at(x):
    return lax.rem(48 * lax.axis_index("gx") + 12 * x + 80, LANES)


def within(x, first, end, shape):
    place = (lanes_of(shape) + (LANES - base_at(x) - first)) & (LANES - 1)
    return place < end - first


def towards(sign):
    return [c for c in range(NFLOW) if MOVING[c][0] == sign]


def start_kernel(flow_in, species_in, fluid_in, react_in, block_ref, right_ref, left_ref, flow_ref, species_ref, fluid_ref, react_ref, done):
    pairs = ((flow_in, flow_ref), (species_in, species_ref), (fluid_in, fluid_ref), (react_in, react_ref))
    copies = [pltpu.make_async_copy(one, two, done.at[k]) for k, (one, two) in enumerate(pairs)]
    for copy in copies:
        copy.start()
    for copy in copies:
        copy.wait()
    for x in range(DEEP):
        turn = lax.rem(base_at(DEEP + x) + 8, LANES)
        fluid = fluid_ref[x].astype(jnp.float32)
        react = react_ref[x].astype(jnp.float32)
        flow = [flow_ref[k, x] * fluid for k in range(10)]
        species = [species_ref[k, x] * fluid for k in range(4)]
        post = collide(flow, species)
        for far, sign, ref in ((0, 1, right_ref), (3, -1, left_ref)):
            if x == far:
                _, flow_pops = flow_populations(post[:10])
                _, species_pops = species_populations(post[10:])
                parts = [flow_pops[c] for c in towards(sign)] + [species_pops[towards(sign)[0]], fluid]
                parts[0] = jnp.where(fluid > 0.5, parts[0], react)
                for k, value in enumerate(parts):
                    ref[NEAR + k] = roll(value, turn, 1)
        post[0] = jnp.where(fluid > 0.5, post[0], react)
        for k, value in enumerate(post + [fluid]):
            value = roll(value, turn, 1)
            block_ref[k, x] = value
            if x > 0:
                right_ref[3 * k + x - 1] = value
            if x < 3:
                left_ref[3 * k + x] = value


def put_rows(up_ref, down_ref, place, one, two):
    high = rows_of((ROWS, LANES)) >= 4
    two = roll(two, 4, 0)
    up_ref[place] = jnp.where(high, one, two)
    down_ref[place] = jnp.where(high, two, one)


def layer_of(field, x, own_ref, left_ref, right_ref):
    if x < 4:
        return left_ref[3 * field + x - 1]
    if x < 8:
        return own_ref[field, x - 4]
    return right_ref[3 * field + x - 8]


def own_rows_kernel(block_in, block_ref, up_ref, down_ref, done):
    copy = pltpu.make_async_copy(block_in, block_ref, done)
    copy.start()
    copy.wait()
    for field in range(FIELDS):
        for k in range(2):
            put_rows(up_ref, down_ref, 2 * field + k, block_ref[field, k], block_ref[field, k + 2])


def rows_kernel(left_ref, right_ref, own_up, own_down, up_ref, down_ref):
    for k in range(HALF):
        put_rows(up_ref, down_ref, k, left_ref[k], right_ref[k])


TALL = (2 * ROWS, LANES)


def halves(up_ref, down_ref, place):
    low = rows_of((ROWS, LANES)) < 4
    up, down = up_ref[place], down_ref[place]
    return jnp.where(low, down, up), roll(jnp.where(low, up, down), 4, 0)


def layer_of(field, x, own_ref, left_ref, right_ref):
    if x < 4:
        return left_ref[3 * field + x - 1]
    if x < 8:
        return own_ref[field, x - 4]
    return right_ref[3 * field + x - 8]


def rows_beyond(field, own_up, own_down, up_ref, down_ref):
    found = {}
    for k in range(2):
        found[4 + k], found[6 + k] = halves(own_up, own_down, 2 * field + k)
    for k in range(3):
        found[1 + k], found[8 + k] = halves(up_ref, down_ref, 3 * field + k)
    return found


def edges_kernel(own_ref, left_ref, right_ref, own_up, own_down, up_ref, down_ref, edge_ref):
    refs = (own_ref, left_ref, right_ref)
    here = [within(x, 4, 12, (ROWS, LANES)) for x in range(12)]
    for field in range(FIELDS):
        near = jnp.zeros((ROWS, LANES), jnp.float32)
        beyond = near
        for x, value in rows_beyond(field, own_up, own_down, up_ref, down_ref).items():
            near = jnp.where(here[x], layer_of(field, x, *refs), near)
            beyond = jnp.where(here[x], value, beyond)
        if field < 14:
            x, ref = ((0, left_ref), (11, right_ref))[field // 7]
            value = halves(up_ref, down_ref, FAR_ROWS + field % 7)[field // 7]
            near = jnp.where(here[x], ref[NEAR + field % 7], near)
            beyond = jnp.where(here[x], value, beyond)
        edge_ref[field, 0:ROWS] = near
        edge_ref[field, ROWS : 2 * ROWS] = beyond


def marked(first, conc, fluid):
    solid = fluid < 0.5
    mark = jnp.where(first > 0.5, REACTIVE, SOLID)
    return jnp.where(solid, SOLID, first), jnp.where(solid, mark, conc)


def marked_far(parts):
    solid = parts[6] < 0.5
    mark = jnp.where(parts[0] > 0.5, REACTIVE, SOLID)
    return [jnp.where(solid, SOLID, part) for part in parts[:5]] + [jnp.where(solid, mark, parts[5])]


def moved(value, c):
    cx, cy, cz = MOVING[c]
    return roll(roll(value, 12 * cx + cz, 1), cy, 0)


def send(state_ref, sent_ref, x):
    _, flow_pops = flow_populations([state_ref[k, x] for k in range(10)])
    _, species_pops = species_populations([state_ref[k, x] for k in range(10, 14)])
    for c in range(NFLOW):
        sent_ref[c, x] = moved(flow_pops[c], c)
    for c in range(NSPEC):
        sent_ref[NFLOW + c, x] = moved(species_pops[c], c)


def release(arriving_species):
    parts = [value[0:ROWS] for value in arriving_species]
    parts = [jnp.where(is_number(part), SPECIES_WEIGHT - part, 0.0) for part in parts]
    return (parts[0] + parts[1]) + (parts[2] + parts[3]) + (parts[4] + parts[5])


def results(post, flow, species, released):
    fluid = is_number(post[0])
    out = [jnp.where(fluid, value, 0.0) for value in flow + species]
    return out + [jnp.where(post[10] > LARGEST, REACT_RATE * released, 0.0)]


def layers_kernel(
    own_ref, left_ref, right_ref, own_up, own_down, up_ref, down_ref, result_ref, near_ref, far_ref, state, sent
):
    refs = (own_ref, left_ref, right_ref)
    for field in range(FIELDS):
        for x, value in rows_beyond(field, own_up, own_down, up_ref, down_ref).items():
            state[field, x, 0:ROWS] = layer_of(field, x, *refs)
            state[field, x, ROWS : 2 * ROWS] = value
    for x in range(1, 11):
        rho, conc = marked(state[0, x], state[10, x], state[FLUID, x])
        state[0, x] = rho
        state[10, x] = conc
    for side in range(2):
        own = [within(x, 0, 8, TALL) if side else within(x, 8, 16, TALL) for x in range(1, 11)]
        for field in range(14):
            near = jnp.full(TALL, SOLID if field in (0, 10) else 0.0, jnp.float32)
            for x in range(1, 11):
                near = jnp.where(own[x - 1], state[field, x], near)
            near_ref[side, field] = near
    beyond = [halves(up_ref, down_ref, FAR_ROWS + k) for k in range(7)]
    for end, (x, sign, ref) in enumerate(((0, 1, left_ref), (11, -1, right_ref))):
        parts = marked_far([jnp.concatenate([ref[NEAR + k], beyond[k][end]]) for k in range(7)])
        along = towards(sign)
        for k, c in enumerate(along):
            sent[c, x] = moved(parts[k], c)
        sent[NFLOW + along[0], x] = moved(parts[5], along[0])
        for k in range(6):
            far_ref[end, k] = parts[k]
    released = [jnp.zeros((ROWS, LANES), jnp.float32)] * DEEP
    for step in range(STEPS):
        last = step == STEPS - 1
        for x in range(max(step, 1), 12 - max(step, 1)):
            send(state, sent, x)
        height = ROWS if last else 2 * ROWS
        for x in range(step + 1, 11 - step):
            post = [state[k, x, 0:height] for k in range(14)]
            arriving = [sent[c, x - MOVING[c][0], 0:height] for c in range(NFLOW)]
            arriving_species = [sent[NFLOW + c, x - MOVING[c][0], 0:height] for c in range(NSPEC)]
            new_flow, new_species = pass_on(post, arriving, arriving_species)
            own = x - DEEP
            if 0 <= own < DEEP:
                released[own] = released[own] + release(arriving_species)
            if last:
                for k, value in enumerate(results(post, new_flow, new_species, released[own])):
                    result_ref[k, own] = value
            else:
                for k, value in enumerate(next_post(post, new_flow, new_species)):
                    state[k, x] = value


def strips_kernel(result_ref, near_ref, far_ref, below_ref, above_ref, flow_out, species_out, dissolved_out, strips):
    for side, ref in enumerate((below_ref, above_ref)):
        first = 0 if side else 4
        place = (lanes_of(TALL) + (LANES - base_at(1) - first)) & (LANES - 1)
        place = place - 12 * ((place * 43) >> 9)
        outside = place >= 8 if side else place < 4
        rho, conc = marked(ref[0], ref[10], ref[FLUID])
        post = [jnp.where(outside, rho if k == 0 else conc if k == 10 else ref[k], near_ref[side, k]) for k in range(14)]
        released = jnp.zeros((ROWS, LANES), jnp.float32)
        for step in range(STEPS):
            last = step == STEPS - 1
            _, flow_pops = flow_populations(post[:10])
            _, species_pops = species_populations(post[10:])
            arriving = [moved(flow_pops[c], c) for c in range(NFLOW)]
            arriving_species = [moved(species_pops[c], c) for c in range(NSPEC)]
            if step == 0:
                for end, (x, sign) in enumerate(((0, 1), (11, -1))):
                    here = within(x + sign, first, first + 12, TALL)
                    there = within(x, 8, 12, TALL) if side else within(x, 4, 8, TALL)
                    parts = marked_far([ref[7 * end + k] for k in range(7)])
                    parts = [jnp.where(there, part, far_ref[end, k]) for k, part in enumerate(parts)]
                    for k, c in enumerate(towards(sign)):
                        arriving[c] = jnp.where(here, moved(parts[k], c), arriving[c])
                    c = towards(sign)[0]
                    arriving_species[c] = jnp.where(here, moved(parts[5], c), arriving_species[c])
            released = released + release(arriving_species)
            if last:
                post = [value[0:ROWS] for value in post]
                arriving = [value[0:ROWS] for value in arriving]
                arriving_species = [value[0:ROWS] for value in arriving_species]
            new_flow, new_species = pass_on(post, arriving, arriving_species)
            if last:
                for k, value in enumerate(results(post, new_flow, new_species, released)):
                    strips[side, k] = value
            else:
                post = next_post(post, new_flow, new_species)
    for own in range(DEEP):
        x = DEEP + own
        low, high = within(x, 8, 12, (ROWS, LANES)), within(x, 4, 8, (ROWS, LANES))
        back = lax.rem(2 * LANES - 8 - base_at(x), LANES)
        for k in range(15):
            value = jnp.where(low, strips[0, k], jnp.where(high, strips[1, k], result_ref[k, own]))
            value = roll(value, back, 1)
            if k < 10:
                flow_out[k, own] = value
            elif k < 14:
                species_out[k - 10, own] = value
            else:
                dissolved_out[own] = value


def shifted(upward, downward, axis, wrap):
    count = lax.axis_size(axis)
    up = [(i, (i + 1) % count) for i in range(count if wrap else count - 1)]
    down = [(j, i) for i, j in up]
    return lax.ppermute(upward, axis, up), lax.ppermute(downward, axis, down)


def vmem(count):
    return [pl.BlockSpec(memory_space=pltpu.VMEM)] * count


def per_device(flow_moments, species_moments, fluid_mask, reactive_mask):
    f32 = jnp.float32
    small = pltpu.CompilerParams(vmem_limit_bytes=16 * 1024 * 1024)
    half = jax.ShapeDtypeStruct((HALF, ROWS, LANES), f32)
    block, to_right, to_left = pl.pallas_call(
        start_kernel,
        out_shape=(jax.ShapeDtypeStruct((FIELDS, DEEP, ROWS, LANES), f32), half, half),
        in_specs=[pl.BlockSpec(memory_space=pltpu.HBM)] * 4,
        out_specs=tuple(vmem(3)),
        scratch_shapes=[
            pltpu.VMEM(flow_moments.shape, f32),
            pltpu.VMEM(species_moments.shape, f32),
            pltpu.VMEM(fluid_mask.shape, fluid_mask.dtype),
            pltpu.VMEM(reactive_mask.shape, reactive_mask.dtype),
            pltpu.SemaphoreType.DMA((4,)),
        ],
        compiler_params=pltpu.CompilerParams(vmem_limit_bytes=56 * 1024 * 1024),
    )(flow_moments, species_moments, fluid_mask, reactive_mask)
    left, right = shifted(to_right, to_left, "gx", True)
    own_tiles = jax.ShapeDtypeStruct((OWN_TILES, ROWS, LANES), f32)
    block, own_to_up, own_to_down = pl.pallas_call(
        own_rows_kernel,
        out_shape=(jax.ShapeDtypeStruct(block.shape, f32), own_tiles, own_tiles),
        in_specs=[pl.BlockSpec(memory_space=pltpu.HBM)],
        out_specs=tuple(vmem(3)),
        scratch_shapes=[pltpu.SemaphoreType.DMA],
        compiler_params=small,
        cost_estimate=pl.CostEstimate(flops=10**7, bytes_accessed=10**7, transcendentals=0),
    )(block)
    own_rows = shifted(own_to_up, own_to_down, "gy", False)
    tiles = jax.ShapeDtypeStruct((HALF, ROWS, LANES), f32)
    to_up, to_down = pl.pallas_call(
        rows_kernel,
        out_shape=(tiles, tiles),
        in_specs=vmem(2) + [pl.BlockSpec(memory_space=pl.ANY)] * 2,
        out_specs=tuple(vmem(2)),
        compiler_params=small,
    )(left, right, *own_rows)
    rows = own_rows + shifted(to_up, to_down, "gy", False)
    strips = jax.ShapeDtypeStruct((FIELDS,) + TALL, f32)
    edge = pl.pallas_call(
        edges_kernel,
        out_shape=strips,
        in_specs=vmem(7),
        out_specs=vmem(1)[0],
        compiler_params=small,
    )(block, left, right, *rows)
    below, above = shifted(edge, edge, "gz", False)
    result, near, far = pl.pallas_call(
        layers_kernel,
        out_shape=(
            jax.ShapeDtypeStruct((15, DEEP, ROWS, LANES), f32),
            jax.ShapeDtypeStruct((2, 14) + TALL, f32),
            jax.ShapeDtypeStruct((2, 6) + TALL, f32),
        ),
        in_specs=vmem(7),
        out_specs=tuple(vmem(3)),
        scratch_shapes=[
            pltpu.VMEM((FIELDS, 12) + TALL, f32),
            pltpu.VMEM((NFLOW + NSPEC, 12) + TALL, f32),
        ],
        compiler_params=small,
        cost_estimate=pl.CostEstimate(flops=10**7, bytes_accessed=10**7, transcendentals=0),
    )(block, left, right, *rows)
    return pl.pallas_call(
        strips_kernel,
        out_shape=(
            jax.ShapeDtypeStruct(flow_moments.shape, f32),
            jax.ShapeDtypeStruct(species_moments.shape, f32),
            jax.ShapeDtypeStruct(fluid_mask.shape, f32),
        ),
        in_specs=vmem(5),
        out_specs=tuple(vmem(3)),
        scratch_shapes=[pltpu.VMEM((2, 15, ROWS, LANES), f32)],
        compiler_params=small,
    )(result, near, far, below, above)


def solution(mesh):
    return jax.shard_map(
        per_device,
        mesh=mesh,
        in_specs=(
            P(None, "gx", "gy", "gz"),
            P(None, "gx", "gy", "gz"),
            P("gx", "gy", "gz"),
            P("gx", "gy", "gz"),
        ),
        out_specs=(P(None, "gx", "gy", "gz"), P(None, "gx", "gy", "gz"), P("gx", "gy", "gz")),
        check_vma=False,
    )
```

```python
import jax
import jax.numpy as jnp
from jax import lax
from jax.experimental import pallas as pl
from jax.experimental.pallas import tpu as pltpu
from jax.sharding import PartitionSpec as P

STEPS = 4
DEEP = 4
KEEP_FLOW = 1.0 - 1.0 / 0.8
KEEP_SPECIES = 1.0 - 1.0 / 0.7
REACT_RATE = 0.5
GRAVITY = 0.001
MOVING = [
    (1, 0, 0),
    (-1, 0, 0),
    (0, 1, 0),
    (0, -1, 0),
    (0, 0, 1),
    (0, 0, -1),
    (1, 1, 0),
    (-1, -1, 0),
    (1, -1, 0),
    (-1, 1, 0),
    (1, 0, 1),
    (-1, 0, -1),
    (1, 0, -1),
    (-1, 0, 1),
    (0, 1, 1),
    (0, -1, -1),
    (0, 1, -1),
    (0, -1, 1),
]
NFLOW = 18
NSPEC = 6
SPECIES_WEIGHT = 0.125
FIELDS = 15
FLUID = 14
NEAR = 3 * FIELDS
HALF = 45 + 7
OWN_TILES = 2 * FIELDS
FAR_ROWS = 3 * FIELDS
ROWS = 8
LANES = 128
SOLID = float("nan")
REACTIVE = float("inf")
LARGEST = 3.0e38


def opposite(index):
    return index ^ 1


def flow_populations(m):
    third = m[0] * (1.0 / 3.0)
    axx, ayy, azz = m[4] - third, m[5] - third, m[6] - third
    base = m[0] - 1.5 * (axx + ayy + azz)
    sides = (4.5 * axx, 4.5 * ayy, 4.5 * azz)
    drift = [m[1 + k] * (1.0 / 12.0) for k in range(3)]
    moving = []
    lifted = [base + side for side in sides]
    for k in range(3):
        even, odd = lifted[k] * (1.0 / 18.0), m[1 + k] * (1.0 / 6.0)
        moving += [even + odd, even - odd]
    for a, b, cross in ((0, 1, 7), (0, 2, 8), (1, 2, 9)):
        both = (lifted[a] + sides[b]) * (1.0 / 36.0)
        mixed = m[cross] * 0.25
        same, differ = both + mixed, both - mixed
        plus, minus = drift[a] + drift[b], drift[a] - drift[b]
        moving += [same + plus, same - plus, differ + minus, differ - minus]
    return base * (1.0 / 3.0), moving


def species_populations(s):
    part = s[0] * SPECIES_WEIGHT
    moving = []
    for k in range(3):
        odd = s[1 + k] * 0.5
        moving += [part + odd, part - odd]
    return s[0] * 0.25, moving


def collide(flow, species):
    rho = flow[0]
    j = flow[1:4]
    third = rho * (1.0 / 3.0)
    equil = [third + j[0] * j[0], third + j[1] * j[1], third + j[2] * j[2], j[0] * j[1], j[0] * j[2], j[1] * j[2]]
    stress = [KEEP_FLOW * flow[4 + k] + (1.0 - KEEP_FLOW) * equil[k] for k in range(6)]
    conc = species[0]
    flux = [KEEP_SPECIES * species[1 + k] + (1.0 - KEEP_SPECIES) * (conc * j[k]) for k in range(3)]
    return [rho] + list(j) + stress + [conc] + flux


def is_number(value):
    return value < LARGEST


def pass_on(post, arriving, arriving_species):
    rest, own = flow_populations(post[:10])
    f = []
    for c in range(NFLOW):
        value = arriving[c]
        f.append(jnp.where(is_number(value), value, own[opposite(c)]))
    total = [f[2 * k] + f[2 * k + 1] for k in range(9)]
    diff = [f[2 * k] - f[2 * k + 1] for k in range(9)]
    xy, xz, yz = total[3] + total[4], total[5] + total[6], total[7] + total[8]
    rho = rest + (total[0] + total[1] + total[2]) + (xy + xz + yz)
    jx = diff[0] + (diff[3] + diff[4]) + (diff[5] + diff[6]) + GRAVITY
    jy = diff[1] + (diff[3] - diff[4]) + (diff[7] + diff[8])
    jz = diff[2] + (diff[5] - diff[6]) + (diff[7] - diff[8])
    flow = [
        rho,
        jx,
        jy,
        jz,
        total[0] + xy + xz,
        total[1] + xy + yz,
        total[2] + xz + yz,
        total[3] - total[4],
        total[5] - total[6],
        total[7] - total[8],
    ]
    rest, own = species_populations(post[10:14])
    g = []
    for c in range(NSPEC):
        value = arriving_species[c]
        back = own[opposite(c)]
        slow = jnp.where(value > LARGEST, REACT_RATE, 0.0)
        g.append(jnp.where(is_number(value), value, back + slow * (SPECIES_WEIGHT - back)))
    conc = rest + (g[0] + g[1]) + (g[2] + g[3]) + (g[4] + g[5])
    return flow, [conc, g[0] - g[1], g[2] - g[3], g[4] - g[5]]


def next_post(post, flow, species):
    fluid = is_number(post[0])
    new = collide(flow, species)
    new[0] = jnp.where(fluid, new[0], post[0])
    new[10] = jnp.where(fluid, new[10], post[10])
    for k in range(11, 14):
        new[k] = jnp.where(fluid, new[k], 0.0)
    return new


def lanes_of(shape):
    return lax.broadcasted_iota(jnp.int32, shape, len(shape) - 1)


def rows_of(shape):
    return lax.broadcasted_iota(jnp.int32, shape, len(shape) - 2)


def roll(value, shift, axis):
    size = value.shape[axis]
    if isinstance(shift, int):
        shift = shift % size
        if shift == 0:
            return value
    return pltpu.roll(value, shift, axis)


def base_at(x):
    return lax.rem(48 * lax.axis_index("gx") + 12 * x + 80, LANES)


def within(x, first, end, shape):
    place = (lanes_of(shape) + (LANES - base_at(x) - first)) & (LANES - 1)
    return place < end - first


def towards(sign):
    return [c for c in range(NFLOW) if MOVING[c][0] == sign]


def start_kernel(inputs_ref, block_ref, right_ref, left_ref):
    for x in range(DEEP):
        turn = lax.rem(base_at(DEEP + x) + 8, LANES)
        fluid, react = inputs_ref[14, x], inputs_ref[15, x]
        flow = [inputs_ref[k, x] * fluid for k in range(10)]
        species = [inputs_ref[k, x] * fluid for k in range(10, 14)]
        post = collide(flow, species)
        for far, sign, ref in ((0, 1, right_ref), (3, -1, left_ref)):
            if x == far:
                _, flow_pops = flow_populations(post[:10])
                _, species_pops = species_populations(post[10:])
                parts = [flow_pops[c] for c in towards(sign)] + [species_pops[towards(sign)[0]], fluid]
                parts[0] = jnp.where(fluid > 0.5, parts[0], react)
                for k, value in enumerate(parts):
                    ref[NEAR + k] = roll(value, turn, 1)
        post[0] = jnp.where(fluid > 0.5, post[0], react)
        for k, value in enumerate(post + [fluid]):
            value = roll(value, turn, 1)
            block_ref[k, x] = value
            if x > 0:
                right_ref[3 * k + x - 1] = value
            if x < 3:
                left_ref[3 * k + x] = value


def put_rows(up_ref, down_ref, place, one, two):
    high = rows_of((ROWS, LANES)) >= 4
    two = roll(two, 4, 0)
    up_ref[place] = jnp.where(high, one, two)
    down_ref[place] = jnp.where(high, two, one)


def layer_of(field, x, own_ref, left_ref, right_ref):
    if x < 4:
        return left_ref[3 * field + x - 1]
    if x < 8:
        return own_ref[field, x - 4]
    return right_ref[3 * field + x - 8]


def own_rows_kernel(block_in, block_ref, up_ref, down_ref, done):
    copy = pltpu.make_async_copy(block_in, block_ref, done)
    copy.start()
    copy.wait()
    for field in range(FIELDS):
        for k in range(2):
            put_rows(up_ref, down_ref, 2 * field + k, block_ref[field, k], block_ref[field, k + 2])


def rows_kernel(left_ref, right_ref, own_up, own_down, up_ref, down_ref):
    for k in range(HALF):
        put_rows(up_ref, down_ref, k, left_ref[k], right_ref[k])


TALL = (2 * ROWS, LANES)


def halves(up_ref, down_ref, place):
    low = rows_of((ROWS, LANES)) < 4
    up, down = up_ref[place], down_ref[place]
    return jnp.where(low, down, up), roll(jnp.where(low, up, down), 4, 0)


def layer_of(field, x, own_ref, left_ref, right_ref):
    if x < 4:
        return left_ref[3 * field + x - 1]
    if x < 8:
        return own_ref[field, x - 4]
    return right_ref[3 * field + x - 8]


def rows_beyond(field, own_up, own_down, up_ref, down_ref):
    found = {}
    for k in range(2):
        found[4 + k], found[6 + k] = halves(own_up, own_down, 2 * field + k)
    for k in range(3):
        found[1 + k], found[8 + k] = halves(up_ref, down_ref, 3 * field + k)
    return found


def edges_kernel(own_ref, left_ref, right_ref, own_up, own_down, up_ref, down_ref, edge_ref):
    refs = (own_ref, left_ref, right_ref)
    here = [within(x, 4, 12, (ROWS, LANES)) for x in range(12)]
    for field in range(FIELDS):
        near = jnp.zeros((ROWS, LANES), jnp.float32)
        beyond = near
        for x, value in rows_beyond(field, own_up, own_down, up_ref, down_ref).items():
            near = jnp.where(here[x], layer_of(field, x, *refs), near)
            beyond = jnp.where(here[x], value, beyond)
        if field < 14:
            x, ref = ((0, left_ref), (11, right_ref))[field // 7]
            value = halves(up_ref, down_ref, FAR_ROWS + field % 7)[field // 7]
            near = jnp.where(here[x], ref[NEAR + field % 7], near)
            beyond = jnp.where(here[x], value, beyond)
        edge_ref[field, 0:ROWS] = near
        edge_ref[field, ROWS : 2 * ROWS] = beyond


def marked(first, conc, fluid):
    solid = fluid < 0.5
    mark = jnp.where(first > 0.5, REACTIVE, SOLID)
    return jnp.where(solid, SOLID, first), jnp.where(solid, mark, conc)


def marked_far(parts):
    solid = parts[6] < 0.5
    mark = jnp.where(parts[0] > 0.5, REACTIVE, SOLID)
    return [jnp.where(solid, SOLID, part) for part in parts[:5]] + [jnp.where(solid, mark, parts[5])]


def moved(value, c):
    cx, cy, cz = MOVING[c]
    return roll(roll(value, 12 * cx + cz, 1), cy, 0)


def send(state_ref, sent_ref, x):
    _, flow_pops = flow_populations([state_ref[k, x] for k in range(10)])
    _, species_pops = species_populations([state_ref[k, x] for k in range(10, 14)])
    for c in range(NFLOW):
        sent_ref[c, x] = moved(flow_pops[c], c)
    for c in range(NSPEC):
        sent_ref[NFLOW + c, x] = moved(species_pops[c], c)


def release(arriving_species):
    parts = [value[0:ROWS] for value in arriving_species]
    parts = [jnp.where(is_number(part), SPECIES_WEIGHT - part, 0.0) for part in parts]
    return (parts[0] + parts[1]) + (parts[2] + parts[3]) + (parts[4] + parts[5])


def results(post, flow, species, released):
    fluid = is_number(post[0])
    out = [jnp.where(fluid, value, 0.0) for value in flow + species]
    return out + [jnp.where(post[10] > LARGEST, REACT_RATE * released, 0.0)]


def layers_kernel(
    own_ref, left_ref, right_ref, own_up, own_down, up_ref, down_ref, result_ref, near_ref, far_ref, state, sent
):
    refs = (own_ref, left_ref, right_ref)
    for field in range(FIELDS):
        for x, value in rows_beyond(field, own_up, own_down, up_ref, down_ref).items():
            state[field, x, 0:ROWS] = layer_of(field, x, *refs)
            state[field, x, ROWS : 2 * ROWS] = value
    for x in range(1, 11):
        rho, conc = marked(state[0, x], state[10, x], state[FLUID, x])
        state[0, x] = rho
        state[10, x] = conc
    for side in range(2):
        own = [within(x, 0, 8, TALL) if side else within(x, 8, 16, TALL) for x in range(1, 11)]
        for field in range(14):
            near = jnp.full(TALL, SOLID if field in (0, 10) else 0.0, jnp.float32)
            for x in range(1, 11):
                near = jnp.where(own[x - 1], state[field, x], near)
            near_ref[side, field] = near
    beyond = [halves(up_ref, down_ref, FAR_ROWS + k) for k in range(7)]
    for end, (x, sign, ref) in enumerate(((0, 1, left_ref), (11, -1, right_ref))):
        parts = marked_far([jnp.concatenate([ref[NEAR + k], beyond[k][end]]) for k in range(7)])
        along = towards(sign)
        for k, c in enumerate(along):
            sent[c, x] = moved(parts[k], c)
        sent[NFLOW + along[0], x] = moved(parts[5], along[0])
        for k in range(6):
            far_ref[end, k] = parts[k]
    released = [jnp.zeros((ROWS, LANES), jnp.float32)] * DEEP
    for step in range(STEPS):
        last = step == STEPS - 1
        for x in range(max(step, 1), 12 - max(step, 1)):
            send(state, sent, x)
        height = ROWS if last else 2 * ROWS
        for x in range(step + 1, 11 - step):
            post = [state[k, x, 0:height] for k in range(14)]
            arriving = [sent[c, x - MOVING[c][0], 0:height] for c in range(NFLOW)]
            arriving_species = [sent[NFLOW + c, x - MOVING[c][0], 0:height] for c in range(NSPEC)]
            new_flow, new_species = pass_on(post, arriving, arriving_species)
            own = x - DEEP
            if 0 <= own < DEEP:
                released[own] = released[own] + release(arriving_species)
            if last:
                for k, value in enumerate(results(post, new_flow, new_species, released[own])):
                    result_ref[k, own] = value
            else:
                for k, value in enumerate(next_post(post, new_flow, new_species)):
                    state[k, x] = value


def strips_kernel(result_ref, near_ref, far_ref, below_ref, above_ref, flow_out, species_out, dissolved_out, strips):
    firsts, posts, fars = (4, 0), [], []
    for side, ref in enumerate((below_ref, above_ref)):
        place = (lanes_of(TALL) + (LANES - base_at(1) - firsts[side])) & (LANES - 1)
        place = place - 12 * ((place * 43) >> 9)
        outside = place >= 8 if side else place < 4
        rho, conc = marked(ref[0], ref[10], ref[FLUID])
        marks = {0: rho, 10: conc}
        posts.append([jnp.where(outside, marks[k] if k in marks else ref[k], near_ref[side, k]) for k in range(14)])
        for end, x in enumerate((0, 11)):
            there = within(x, 8, 12, TALL) if side else within(x, 4, 8, TALL)
            parts = marked_far([ref[7 * end + k] for k in range(7)])
            fars.append([jnp.where(there, part, far_ref[end, k]) for k, part in enumerate(parts)])
    released = [jnp.zeros((ROWS, LANES), jnp.float32)] * 2
    for step in range(STEPS):
        last = step == STEPS - 1
        for side in range(2):
            post = posts[side]
            _, flow_pops = flow_populations(post[:10])
            _, species_pops = species_populations(post[10:])
            arriving = [moved(flow_pops[c], c) for c in range(NFLOW)]
            arriving_species = [moved(species_pops[c], c) for c in range(NSPEC)]
            if step == 0:
                for end, (x, sign) in enumerate(((0, 1), (11, -1))):
                    here = within(x + sign, firsts[side], firsts[side] + 12, TALL)
                    parts = fars[2 * side + end]
                    for k, c in enumerate(towards(sign)):
                        arriving[c] = jnp.where(here, moved(parts[k], c), arriving[c])
                    c = towards(sign)[0]
                    arriving_species[c] = jnp.where(here, moved(parts[5], c), arriving_species[c])
            released[side] = released[side] + release(arriving_species)
            if last:
                post = [value[0:ROWS] for value in post]
                arriving = [value[0:ROWS] for value in arriving]
                arriving_species = [value[0:ROWS] for value in arriving_species]
            new_flow, new_species = pass_on(post, arriving, arriving_species)
            if last:
                for k, value in enumerate(results(post, new_flow, new_species, released[side])):
                    strips[side, k] = value
            else:
                posts[side] = next_post(post, new_flow, new_species)
    for own in range(DEEP):
        x = DEEP + own
        low, high = within(x, 8, 12, (ROWS, LANES)), within(x, 4, 8, (ROWS, LANES))
        back = lax.rem(2 * LANES - 8 - base_at(x), LANES)
        for k in range(15):
            value = jnp.where(low, strips[0, k], jnp.where(high, strips[1, k], result_ref[k, own]))
            value = roll(value, back, 1)
            if k < 10:
                flow_out[k, own] = value
            elif k < 14:
                species_out[k - 10, own] = value
            else:
                dissolved_out[own] = value


def shifted(upward, downward, axis, wrap):
    count = lax.axis_size(axis)
    up = [(i, (i + 1) % count) for i in range(count if wrap else count - 1)]
    down = [(j, i) for i, j in up]
    return lax.ppermute(upward, axis, up), lax.ppermute(downward, axis, down)


def vmem(count):
    return [pl.BlockSpec(memory_space=pltpu.VMEM)] * count


def per_device(flow_moments, species_moments, fluid_mask, reactive_mask):
    f32 = jnp.float32
    small = pltpu.CompilerParams(vmem_limit_bytes=16 * 1024 * 1024)
    masks = [mask.astype(f32)[None] for mask in (fluid_mask, reactive_mask)]
    inputs = jnp.concatenate([flow_moments, species_moments] + masks)
    half = jax.ShapeDtypeStruct((HALF, ROWS, LANES), f32)
    block, to_right, to_left = pl.pallas_call(
        start_kernel,
        out_shape=(jax.ShapeDtypeStruct((FIELDS, DEEP, ROWS, LANES), f32), half, half),
        in_specs=vmem(1),
        out_specs=tuple(vmem(3)),
        compiler_params=small,
    )(inputs)
    left, right = shifted(to_right, to_left, "gx", True)
    own_tiles = jax.ShapeDtypeStruct((OWN_TILES, ROWS, LANES), f32)
    block, own_to_up, own_to_down = pl.pallas_call(
        own_rows_kernel,
        out_shape=(jax.ShapeDtypeStruct(block.shape, f32), own_tiles, own_tiles),
        in_specs=[pl.BlockSpec(memory_space=pltpu.HBM)],
        out_specs=tuple(vmem(3)),
        scratch_shapes=[pltpu.SemaphoreType.DMA],
        compiler_params=small,
        cost_estimate=pl.CostEstimate(flops=10**7, bytes_accessed=10**7, transcendentals=0),
    )(block)
    own_rows = shifted(own_to_up, own_to_down, "gy", False)
    tiles = jax.ShapeDtypeStruct((HALF, ROWS, LANES), f32)
    to_up, to_down = pl.pallas_call(
        rows_kernel,
        out_shape=(tiles, tiles),
        in_specs=vmem(2) + [pl.BlockSpec(memory_space=pl.ANY)] * 2,
        out_specs=tuple(vmem(2)),
        compiler_params=small,
    )(left, right, *own_rows)
    rows = own_rows + shifted(to_up, to_down, "gy", False)
    strips = jax.ShapeDtypeStruct((FIELDS,) + TALL, f32)
    edge = pl.pallas_call(
        edges_kernel,
        out_shape=strips,
        in_specs=vmem(7),
        out_specs=vmem(1)[0],
        compiler_params=small,
    )(block, left, right, *rows)
    below, above = shifted(edge, edge, "gz", False)
    result, near, far = pl.pallas_call(
        layers_kernel,
        out_shape=(
            jax.ShapeDtypeStruct((15, DEEP, ROWS, LANES), f32),
            jax.ShapeDtypeStruct((2, 14) + TALL, f32),
            jax.ShapeDtypeStruct((2, 6) + TALL, f32),
        ),
        in_specs=vmem(7),
        out_specs=tuple(vmem(3)),
        scratch_shapes=[
            pltpu.VMEM((FIELDS, 12) + TALL, f32),
            pltpu.VMEM((NFLOW + NSPEC, 12) + TALL, f32),
        ],
        compiler_params=small,
        cost_estimate=pl.CostEstimate(flops=10**7, bytes_accessed=10**7, transcendentals=0),
    )(block, left, right, *rows)
    return pl.pallas_call(
        strips_kernel,
        out_shape=(
            jax.ShapeDtypeStruct(flow_moments.shape, f32),
            jax.ShapeDtypeStruct(species_moments.shape, f32),
            jax.ShapeDtypeStruct(fluid_mask.shape, f32),
        ),
        in_specs=vmem(5),
        out_specs=tuple(vmem(3)),
        scratch_shapes=[pltpu.VMEM((2, 15, ROWS, LANES), f32)],
        compiler_params=small,
    )(result, near, far, below, above)


def solution(mesh):
    return jax.shard_map(
        per_device,
        mesh=mesh,
        in_specs=(
            P(None, "gx", "gy", "gz"),
            P(None, "gx", "gy", "gz"),
            P("gx", "gy", "gz"),
            P("gx", "gy", "gz"),
        ),
        out_specs=(P(None, "gx", "gy", "gz"), P(None, "gx", "gy", "gz"), P("gx", "gy", "gz")),
        check_vma=False,
    )
```

```python
import jax
import jax.numpy as jnp
from jax import lax
from jax.experimental import pallas as pl
from jax.experimental.pallas import tpu as pltpu
from jax.sharding import PartitionSpec as P

STEPS = 4
DEEP = 4
KEEP_FLOW = 1.0 - 1.0 / 0.8
KEEP_SPECIES = 1.0 - 1.0 / 0.7
REACT_RATE = 0.5
GRAVITY = 0.001
MOVING = [
    (1, 0, 0),
    (-1, 0, 0),
    (0, 1, 0),
    (0, -1, 0),
    (0, 0, 1),
    (0, 0, -1),
    (1, 1, 0),
    (-1, -1, 0),
    (1, -1, 0),
    (-1, 1, 0),
    (1, 0, 1),
    (-1, 0, -1),
    (1, 0, -1),
    (-1, 0, 1),
    (0, 1, 1),
    (0, -1, -1),
    (0, 1, -1),
    (0, -1, 1),
]
NFLOW = 18
NSPEC = 6
SPECIES_WEIGHT = 0.125
FIELDS = 15
FLUID = 14
NEAR = 3 * FIELDS
HALF = 45 + 7
OWN_TILES = 2 * FIELDS
FAR_ROWS = 3 * FIELDS
ROWS = 8
LANES = 128
SOLID = float("nan")
REACTIVE = float("inf")
LARGEST = 3.0e38


def opposite(index):
    return index ^ 1


def flow_populations(m):
    third = m[0] * (1.0 / 3.0)
    axx, ayy, azz = m[4] - third, m[5] - third, m[6] - third
    base = m[0] - 1.5 * (axx + ayy + azz)
    sides = (4.5 * axx, 4.5 * ayy, 4.5 * azz)
    drift = [m[1 + k] * (1.0 / 12.0) for k in range(3)]
    moving = []
    lifted = [base + side for side in sides]
    for k in range(3):
        even, odd = lifted[k] * (1.0 / 18.0), m[1 + k] * (1.0 / 6.0)
        moving += [even + odd, even - odd]
    for a, b, cross in ((0, 1, 7), (0, 2, 8), (1, 2, 9)):
        both = (lifted[a] + sides[b]) * (1.0 / 36.0)
        mixed = m[cross] * 0.25
        same, differ = both + mixed, both - mixed
        plus, minus = drift[a] + drift[b], drift[a] - drift[b]
        moving += [same + plus, same - plus, differ + minus, differ - minus]
    return base * (1.0 / 3.0), moving


def species_populations(s):
    part = s[0] * SPECIES_WEIGHT
    moving = []
    for k in range(3):
        odd = s[1 + k] * 0.5
        moving += [part + odd, part - odd]
    return s[0] * 0.25, moving


def collide(flow, species):
    rho = flow[0]
    j = flow[1:4]
    third = rho * (1.0 / 3.0)
    equil = [third + j[0] * j[0], third + j[1] * j[1], third + j[2] * j[2], j[0] * j[1], j[0] * j[2], j[1] * j[2]]
    stress = [KEEP_FLOW * flow[4 + k] + (1.0 - KEEP_FLOW) * equil[k] for k in range(6)]
    conc = species[0]
    flux = [KEEP_SPECIES * species[1 + k] + (1.0 - KEEP_SPECIES) * (conc * j[k]) for k in range(3)]
    return [rho] + list(j) + stress + [conc] + flux


def is_number(value):
    return value < LARGEST


def pass_on(post, arriving, arriving_species):
    rest, own = flow_populations(post[:10])
    f = []
    for c in range(NFLOW):
        value = arriving[c]
        f.append(jnp.where(is_number(value), value, own[opposite(c)]))
    total = [f[2 * k] + f[2 * k + 1] for k in range(9)]
    diff = [f[2 * k] - f[2 * k + 1] for k in range(9)]
    xy, xz, yz = total[3] + total[4], total[5] + total[6], total[7] + total[8]
    rho = rest + (total[0] + total[1] + total[2]) + (xy + xz + yz)
    jx = diff[0] + (diff[3] + diff[4]) + (diff[5] + diff[6]) + GRAVITY
    jy = diff[1] + (diff[3] - diff[4]) + (diff[7] + diff[8])
    jz = diff[2] + (diff[5] - diff[6]) + (diff[7] - diff[8])
    flow = [
        rho,
        jx,
        jy,
        jz,
        total[0] + xy + xz,
        total[1] + xy + yz,
        total[2] + xz + yz,
        total[3] - total[4],
        total[5] - total[6],
        total[7] - total[8],
    ]
    rest, own = species_populations(post[10:14])
    g = []
    for c in range(NSPEC):
        value = arriving_species[c]
        back = own[opposite(c)]
        slow = jnp.where(value > LARGEST, REACT_RATE, 0.0)
        g.append(jnp.where(is_number(value), value, back + slow * (SPECIES_WEIGHT - back)))
    conc = rest + (g[0] + g[1]) + (g[2] + g[3]) + (g[4] + g[5])
    return flow, [conc, g[0] - g[1], g[2] - g[3], g[4] - g[5]]


def next_post(post, flow, species):
    fluid = is_number(post[0])
    new = collide(flow, species)
    new[0] = jnp.where(fluid, new[0], post[0])
    new[10] = jnp.where(fluid, new[10], post[10])
    for k in range(11, 14):
        new[k] = jnp.where(fluid, new[k], 0.0)
    return new


def lanes_of(shape):
    return lax.broadcasted_iota(jnp.int32, shape, len(shape) - 1)


def rows_of(shape):
    return lax.broadcasted_iota(jnp.int32, shape, len(shape) - 2)


def roll(value, shift, axis):
    size = value.shape[axis]
    if isinstance(shift, int):
        shift = shift % size
        if shift == 0:
            return value
    return pltpu.roll(value, shift, axis)


def base_at(x):
    return lax.rem(48 * lax.axis_index("gx") + 12 * x + 80, LANES)


def within(x, first, end, shape):
    place = (lanes_of(shape) + (LANES - base_at(x) - first)) & (LANES - 1)
    return place < end - first


def towards(sign):
    return [c for c in range(NFLOW) if MOVING[c][0] == sign]


def start_kernel(flow_in, species_in, fluid_in, react_in, block_ref, right_ref, left_ref, flow_ref, species_ref, fluid_ref, react_ref, done):
    pairs = ((flow_in, flow_ref), (species_in, species_ref), (fluid_in, fluid_ref), (react_in, react_ref))
    copies = [pltpu.make_async_copy(one, two, done.at[k]) for k, (one, two) in enumerate(pairs)]
    for copy in copies:
        copy.start()
    for copy in copies:
        copy.wait()
    for x in range(DEEP):
        turn = lax.rem(base_at(DEEP + x) + 8, LANES)
        fluid = fluid_ref[x].astype(jnp.float32)
        react = react_ref[x].astype(jnp.float32)
        flow = [flow_ref[k, x] * fluid for k in range(10)]
        species = [species_ref[k, x] * fluid for k in range(4)]
        post = collide(flow, species)
        for far, sign, ref in ((0, 1, right_ref), (3, -1, left_ref)):
            if x == far:
                _, flow_pops = flow_populations(post[:10])
                _, species_pops = species_populations(post[10:])
                parts = [flow_pops[c] for c in towards(sign)] + [species_pops[towards(sign)[0]], fluid]
                parts[0] = jnp.where(fluid > 0.5, parts[0], react)
                for k, value in enumerate(parts):
                    ref[NEAR + k] = roll(value, turn, 1)
        post[0] = jnp.where(fluid > 0.5, post[0], react)
        for k, value in enumerate(post + [fluid]):
            value = roll(value, turn, 1)
            block_ref[k, x] = value
            if x > 0:
                right_ref[3 * k + x - 1] = value
            if x < 3:
                left_ref[3 * k + x] = value


def put_rows(up_ref, down_ref, place, one, two):
    high = rows_of((ROWS, LANES)) >= 4
    two = roll(two, 4, 0)
    up_ref[place] = jnp.where(high, one, two)
    down_ref[place] = jnp.where(high, two, one)


def layer_of(field, x, own_ref, left_ref, right_ref):
    if x < 4:
        return left_ref[3 * field + x - 1]
    if x < 8:
        return own_ref[field, x - 4]
    return right_ref[3 * field + x - 8]


def own_rows_kernel(block_in, block_ref, up_ref, down_ref, done):
    copy = pltpu.make_async_copy(block_in, block_ref, done)
    copy.start()
    copy.wait()
    for field in range(FIELDS):
        for k in range(2):
            put_rows(up_ref, down_ref, 2 * field + k, block_ref[field, k], block_ref[field, k + 2])


def rows_kernel(left_ref, right_ref, own_up, own_down, up_ref, down_ref):
    for k in range(HALF):
        put_rows(up_ref, down_ref, k, left_ref[k], right_ref[k])


TALL = (2 * ROWS, LANES)


def halves(up_ref, down_ref, place):
    low = rows_of((ROWS, LANES)) < 4
    up, down = up_ref[place], down_ref[place]
    return jnp.where(low, down, up), roll(jnp.where(low, up, down), 4, 0)


def layer_of(field, x, own_ref, left_ref, right_ref):
    if x < 4:
        return left_ref[3 * field + x - 1]
    if x < 8:
        return own_ref[field, x - 4]
    return right_ref[3 * field + x - 8]


def rows_beyond(field, own_up, own_down, up_ref, down_ref):
    found = {}
    for k in range(2):
        found[4 + k], found[6 + k] = halves(own_up, own_down, 2 * field + k)
    for k in range(3):
        found[1 + k], found[8 + k] = halves(up_ref, down_ref, 3 * field + k)
    return found


def edges_kernel(own_ref, left_ref, right_ref, own_up, own_down, up_ref, down_ref, edge_ref):
    refs = (own_ref, left_ref, right_ref)
    here = [within(x, 4, 12, (ROWS, LANES)) for x in range(12)]
    for field in range(FIELDS):
        near = jnp.zeros((ROWS, LANES), jnp.float32)
        beyond = near
        for x, value in rows_beyond(field, own_up, own_down, up_ref, down_ref).items():
            near = jnp.where(here[x], layer_of(field, x, *refs), near)
            beyond = jnp.where(here[x], value, beyond)
        if field < 14:
            x, ref = ((0, left_ref), (11, right_ref))[field // 7]
            value = halves(up_ref, down_ref, FAR_ROWS + field % 7)[field // 7]
            near = jnp.where(here[x], ref[NEAR + field % 7], near)
            beyond = jnp.where(here[x], value, beyond)
        edge_ref[field, 0:ROWS] = near
        edge_ref[field, ROWS : 2 * ROWS] = beyond


def marked(first, conc, fluid):
    solid = fluid < 0.5
    mark = jnp.where(first > 0.5, REACTIVE, SOLID)
    return jnp.where(solid, SOLID, first), jnp.where(solid, mark, conc)


def marked_far(parts):
    solid = parts[6] < 0.5
    mark = jnp.where(parts[0] > 0.5, REACTIVE, SOLID)
    return [jnp.where(solid, SOLID, part) for part in parts[:5]] + [jnp.where(solid, mark, parts[5])]


def moved(value, c):
    cx, cy, cz = MOVING[c]
    return roll(roll(value, 12 * cx + cz, 1), cy, 0)


def send(state_ref, sent_ref, x):
    _, flow_pops = flow_populations([state_ref[k, x] for k in range(10)])
    _, species_pops = species_populations([state_ref[k, x] for k in range(10, 14)])
    for c in range(NFLOW):
        sent_ref[c, x] = moved(flow_pops[c], c)
    for c in range(NSPEC):
        sent_ref[NFLOW + c, x] = moved(species_pops[c], c)


def release(arriving_species):
    parts = [value[0:ROWS] for value in arriving_species]
    parts = [jnp.where(is_number(part), SPECIES_WEIGHT - part, 0.0) for part in parts]
    return (parts[0] + parts[1]) + (parts[2] + parts[3]) + (parts[4] + parts[5])


def results(post, flow, species, released):
    fluid = is_number(post[0])
    out = [jnp.where(fluid, value, 0.0) for value in flow + species]
    return out + [jnp.where(post[10] > LARGEST, REACT_RATE * released, 0.0)]


def layers_kernel(
    own_ref, left_ref, right_ref, own_up, own_down, up_ref, down_ref, result_ref, near_ref, far_ref, state, sent
):
    refs = (own_ref, left_ref, right_ref)
    for field in range(FIELDS):
        for x, value in rows_beyond(field, own_up, own_down, up_ref, down_ref).items():
            state[field, x, 0:ROWS] = layer_of(field, x, *refs)
            state[field, x, ROWS : 2 * ROWS] = value
    for x in range(1, 11):
        rho, conc = marked(state[0, x], state[10, x], state[FLUID, x])
        state[0, x] = rho
        state[10, x] = conc
    for side in range(2):
        own = [within(x, 0, 8, TALL) if side else within(x, 8, 16, TALL) for x in range(1, 11)]
        for field in range(14):
            near = jnp.full(TALL, SOLID if field in (0, 10) else 0.0, jnp.float32)
            for x in range(1, 11):
                near = jnp.where(own[x - 1], state[field, x], near)
            near_ref[side, field] = near
    beyond = [halves(up_ref, down_ref, FAR_ROWS + k) for k in range(7)]
    for end, (x, sign, ref) in enumerate(((0, 1, left_ref), (11, -1, right_ref))):
        parts = marked_far([jnp.concatenate([ref[NEAR + k], beyond[k][end]]) for k in range(7)])
        along = towards(sign)
        for k, c in enumerate(along):
            sent[c, x] = moved(parts[k], c)
        sent[NFLOW + along[0], x] = moved(parts[5], along[0])
        for k in range(6):
            far_ref[end, k] = parts[k]
    released = [jnp.zeros((ROWS, LANES), jnp.float32)] * DEEP
    for step in range(STEPS):
        last = step == STEPS - 1
        for x in range(max(step, 1), 12 - max(step, 1)):
            send(state, sent, x)
        height = ROWS if last else 2 * ROWS
        for x in range(step + 1, 11 - step):
            post = [state[k, x, 0:height] for k in range(14)]
            arriving = [sent[c, x - MOVING[c][0], 0:height] for c in range(NFLOW)]
            arriving_species = [sent[NFLOW + c, x - MOVING[c][0], 0:height] for c in range(NSPEC)]
            new_flow, new_species = pass_on(post, arriving, arriving_species)
            own = x - DEEP
            if 0 <= own < DEEP:
                released[own] = released[own] + release(arriving_species)
            if last:
                for k, value in enumerate(results(post, new_flow, new_species, released[own])):
                    result_ref[k, own] = value
            else:
                for k, value in enumerate(next_post(post, new_flow, new_species)):
                    state[k, x] = value


def strips_kernel(result_ref, near_ref, far_ref, below_ref, above_ref, flow_out, species_out, dissolved_out, strips):
    firsts, posts, fars = (4, 0), [], []
    for side, ref in enumerate((below_ref, above_ref)):
        place = (lanes_of(TALL) + (LANES - base_at(1) - firsts[side])) & (LANES - 1)
        place = place - 12 * ((place * 43) >> 9)
        outside = place >= 8 if side else place < 4
        rho, conc = marked(ref[0], ref[10], ref[FLUID])
        marks = {0: rho, 10: conc}
        posts.append([jnp.where(outside, marks[k] if k in marks else ref[k], near_ref[side, k]) for k in range(14)])
        for end, x in enumerate((0, 11)):
            there = within(x, 8, 12, TALL) if side else within(x, 4, 8, TALL)
            parts = marked_far([ref[7 * end + k] for k in range(7)])
            fars.append([jnp.where(there, part, far_ref[end, k]) for k, part in enumerate(parts)])
    released = [jnp.zeros((ROWS, LANES), jnp.float32)] * 2
    for step in range(STEPS):
        last = step == STEPS - 1
        for side in range(2):
            post = posts[side]
            _, flow_pops = flow_populations(post[:10])
            _, species_pops = species_populations(post[10:])
            arriving = [moved(flow_pops[c], c) for c in range(NFLOW)]
            arriving_species = [moved(species_pops[c], c) for c in range(NSPEC)]
            if step == 0:
                for end, (x, sign) in enumerate(((0, 1), (11, -1))):
                    here = within(x + sign, firsts[side], firsts[side] + 12, TALL)
                    parts = fars[2 * side + end]
                    for k, c in enumerate(towards(sign)):
                        arriving[c] = jnp.where(here, moved(parts[k], c), arriving[c])
                    c = towards(sign)[0]
                    arriving_species[c] = jnp.where(here, moved(parts[5], c), arriving_species[c])
            released[side] = released[side] + release(arriving_species)
            if last:
                post = [value[0:ROWS] for value in post]
                arriving = [value[0:ROWS] for value in arriving]
                arriving_species = [value[0:ROWS] for value in arriving_species]
            new_flow, new_species = pass_on(post, arriving, arriving_species)
            if last:
                for k, value in enumerate(results(post, new_flow, new_species, released[side])):
                    strips[side, k] = value
            else:
                posts[side] = next_post(post, new_flow, new_species)
    for own in range(DEEP):
        x = DEEP + own
        low, high = within(x, 8, 12, (ROWS, LANES)), within(x, 4, 8, (ROWS, LANES))
        back = lax.rem(2 * LANES - 8 - base_at(x), LANES)
        for k in range(15):
            value = jnp.where(low, strips[0, k], jnp.where(high, strips[1, k], result_ref[k, own]))
            value = roll(value, back, 1)
            if k < 10:
                flow_out[k, own] = value
            elif k < 14:
                species_out[k - 10, own] = value
            else:
                dissolved_out[own] = value


def shifted(upward, downward, axis, wrap):
    count = lax.axis_size(axis)
    up = [(i, (i + 1) % count) for i in range(count if wrap else count - 1)]
    down = [(j, i) for i, j in up]
    return lax.ppermute(upward, axis, up), lax.ppermute(downward, axis, down)


def vmem(count):
    return [pl.BlockSpec(memory_space=pltpu.VMEM)] * count


def per_device(flow_moments, species_moments, fluid_mask, reactive_mask):
    f32 = jnp.float32
    small = pltpu.CompilerParams(vmem_limit_bytes=16 * 1024 * 1024)
    half = jax.ShapeDtypeStruct((HALF, ROWS, LANES), f32)
    block, to_right, to_left = pl.pallas_call(
        start_kernel,
        out_shape=(jax.ShapeDtypeStruct((FIELDS, DEEP, ROWS, LANES), f32), half, half),
        in_specs=[pl.BlockSpec(memory_space=pltpu.HBM)] * 4,
        out_specs=tuple(vmem(3)),
        scratch_shapes=[
            pltpu.VMEM(flow_moments.shape, f32),
            pltpu.VMEM(species_moments.shape, f32),
            pltpu.VMEM(fluid_mask.shape, fluid_mask.dtype),
            pltpu.VMEM(reactive_mask.shape, reactive_mask.dtype),
            pltpu.SemaphoreType.DMA((4,)),
        ],
        compiler_params=small,
    )(*[pltpu.with_memory_space_constraint(value, pltpu.HBM) for value in (flow_moments, species_moments, fluid_mask, reactive_mask)])
    left, right = shifted(to_right, to_left, "gx", True)
    own_tiles = jax.ShapeDtypeStruct((OWN_TILES, ROWS, LANES), f32)
    block, own_to_up, own_to_down = pl.pallas_call(
        own_rows_kernel,
        out_shape=(jax.ShapeDtypeStruct(block.shape, f32), own_tiles, own_tiles),
        in_specs=[pl.BlockSpec(memory_space=pltpu.HBM)],
        out_specs=tuple(vmem(3)),
        scratch_shapes=[pltpu.SemaphoreType.DMA],
        compiler_params=small,
        cost_estimate=pl.CostEstimate(flops=10**7, bytes_accessed=10**7, transcendentals=0),
    )(block)
    own_rows = shifted(own_to_up, own_to_down, "gy", False)
    tiles = jax.ShapeDtypeStruct((HALF, ROWS, LANES), f32)
    to_up, to_down = pl.pallas_call(
        rows_kernel,
        out_shape=(tiles, tiles),
        in_specs=vmem(2) + [pl.BlockSpec(memory_space=pl.ANY)] * 2,
        out_specs=tuple(vmem(2)),
        compiler_params=small,
    )(left, right, *own_rows)
    rows = own_rows + shifted(to_up, to_down, "gy", False)
    strips = jax.ShapeDtypeStruct((FIELDS,) + TALL, f32)
    edge = pl.pallas_call(
        edges_kernel,
        out_shape=strips,
        in_specs=vmem(7),
        out_specs=vmem(1)[0],
        compiler_params=small,
    )(block, left, right, *rows)
    below, above = shifted(edge, edge, "gz", False)
    result, near, far = pl.pallas_call(
        layers_kernel,
        out_shape=(
            jax.ShapeDtypeStruct((15, DEEP, ROWS, LANES), f32),
            jax.ShapeDtypeStruct((2, 14) + TALL, f32),
            jax.ShapeDtypeStruct((2, 6) + TALL, f32),
        ),
        in_specs=vmem(7),
        out_specs=tuple(vmem(3)),
        scratch_shapes=[
            pltpu.VMEM((FIELDS, 12) + TALL, f32),
            pltpu.VMEM((NFLOW + NSPEC, 12) + TALL, f32),
        ],
        compiler_params=small,
        cost_estimate=pl.CostEstimate(flops=10**7, bytes_accessed=10**7, transcendentals=0),
    )(block, left, right, *rows)
    return pl.pallas_call(
        strips_kernel,
        out_shape=(
            jax.ShapeDtypeStruct(flow_moments.shape, f32),
            jax.ShapeDtypeStruct(species_moments.shape, f32),
            jax.ShapeDtypeStruct(fluid_mask.shape, f32),
        ),
        in_specs=vmem(5),
        out_specs=tuple(vmem(3)),
        scratch_shapes=[pltpu.VMEM((2, 15, ROWS, LANES), f32)],
        compiler_params=small,
    )(result, near, far, below, above)


def solution(mesh):
    return jax.shard_map(
        per_device,
        mesh=mesh,
        in_specs=(
            P(None, "gx", "gy", "gz"),
            P(None, "gx", "gy", "gz"),
            P("gx", "gy", "gz"),
            P("gx", "gy", "gz"),
        ),
        out_specs=(P(None, "gx", "gy", "gz"), P(None, "gx", "gy", "gz"), P("gx", "gy", "gz")),
        check_vma=False,
    )
```

```python
import jax
import jax.numpy as jnp
from jax import lax
from jax.experimental import pallas as pl
from jax.experimental.pallas import tpu as pltpu
from jax.sharding import PartitionSpec as P

STEPS = 4
DEEP = 4
KEEP_FLOW = 1.0 - 1.0 / 0.8
KEEP_SPECIES = 1.0 - 1.0 / 0.7
REACT_RATE = 0.5
GRAVITY = 0.001
MOVING = [
    (1, 0, 0),
    (-1, 0, 0),
    (0, 1, 0),
    (0, -1, 0),
    (0, 0, 1),
    (0, 0, -1),
    (1, 1, 0),
    (-1, -1, 0),
    (1, -1, 0),
    (-1, 1, 0),
    (1, 0, 1),
    (-1, 0, -1),
    (1, 0, -1),
    (-1, 0, 1),
    (0, 1, 1),
    (0, -1, -1),
    (0, 1, -1),
    (0, -1, 1),
]
NFLOW = 18
NSPEC = 6
SPECIES_WEIGHT = 0.125
FIELDS = 15
FLUID = 14
NEAR = 3 * FIELDS
HALF = 45 + 7
OWN_TILES = 2 * FIELDS
FAR_ROWS = 3 * FIELDS
ROWS = 8
LANES = 128
SOLID = float("nan")
REACTIVE = float("inf")
LARGEST = 3.0e38


def opposite(index):
    return index ^ 1


def flow_populations(m):
    third = m[0] * (1.0 / 3.0)
    axx, ayy, azz = m[4] - third, m[5] - third, m[6] - third
    base = m[0] - 1.5 * (axx + ayy + azz)
    sides = (4.5 * axx, 4.5 * ayy, 4.5 * azz)
    drift = [m[1 + k] * (1.0 / 12.0) for k in range(3)]
    moving = []
    lifted = [base + side for side in sides]
    for k in range(3):
        even, odd = lifted[k] * (1.0 / 18.0), m[1 + k] * (1.0 / 6.0)
        moving += [even + odd, even - odd]
    for a, b, cross in ((0, 1, 7), (0, 2, 8), (1, 2, 9)):
        both = (lifted[a] + sides[b]) * (1.0 / 36.0)
        mixed = m[cross] * 0.25
        same, differ = both + mixed, both - mixed
        plus, minus = drift[a] + drift[b], drift[a] - drift[b]
        moving += [same + plus, same - plus, differ + minus, differ - minus]
    return base * (1.0 / 3.0), moving


def species_populations(s):
    part = s[0] * SPECIES_WEIGHT
    moving = []
    for k in range(3):
        odd = s[1 + k] * 0.5
        moving += [part + odd, part - odd]
    return s[0] * 0.25, moving


def collide(flow, species):
    rho = flow[0]
    j = flow[1:4]
    third = rho * (1.0 / 3.0)
    equil = [third + j[0] * j[0], third + j[1] * j[1], third + j[2] * j[2], j[0] * j[1], j[0] * j[2], j[1] * j[2]]
    stress = [KEEP_FLOW * flow[4 + k] + (1.0 - KEEP_FLOW) * equil[k] for k in range(6)]
    conc = species[0]
    flux = [KEEP_SPECIES * species[1 + k] + (1.0 - KEEP_SPECIES) * (conc * j[k]) for k in range(3)]
    return [rho] + list(j) + stress + [conc] + flux


def is_number(value):
    return value < LARGEST


def pass_on(post, arriving, arriving_species):
    rest, own = flow_populations(post[:10])
    f = []
    for c in range(NFLOW):
        value = arriving[c]
        f.append(jnp.where(is_number(value), value, own[opposite(c)]))
    total = [f[2 * k] + f[2 * k + 1] for k in range(9)]
    diff = [f[2 * k] - f[2 * k + 1] for k in range(9)]
    xy, xz, yz = total[3] + total[4], total[5] + total[6], total[7] + total[8]
    rho = rest + (total[0] + total[1] + total[2]) + (xy + xz + yz)
    jx = diff[0] + (diff[3] + diff[4]) + (diff[5] + diff[6]) + GRAVITY
    jy = diff[1] + (diff[3] - diff[4]) + (diff[7] + diff[8])
    jz = diff[2] + (diff[5] - diff[6]) + (diff[7] - diff[8])
    flow = [
        rho,
        jx,
        jy,
        jz,
        total[0] + xy + xz,
        total[1] + xy + yz,
        total[2] + xz + yz,
        total[3] - total[4],
        total[5] - total[6],
        total[7] - total[8],
    ]
    rest, own = species_populations(post[10:14])
    g = []
    for c in range(NSPEC):
        value = arriving_species[c]
        back = own[opposite(c)]
        slow = jnp.where(value > LARGEST, REACT_RATE, 0.0)
        g.append(jnp.where(is_number(value), value, back + slow * (SPECIES_WEIGHT - back)))
    conc = rest + (g[0] + g[1]) + (g[2] + g[3]) + (g[4] + g[5])
    return flow, [conc, g[0] - g[1], g[2] - g[3], g[4] - g[5]]


def next_post(post, flow, species):
    fluid = is_number(post[0])
    new = collide(flow, species)
    new[0] = jnp.where(fluid, new[0], post[0])
    new[10] = jnp.where(fluid, new[10], post[10])
    for k in range(11, 14):
        new[k] = jnp.where(fluid, new[k], 0.0)
    return new


def lanes_of(shape):
    return lax.broadcasted_iota(jnp.int32, shape, len(shape) - 1)


def rows_of(shape):
    return lax.broadcasted_iota(jnp.int32, shape, len(shape) - 2)


def roll(value, shift, axis):
    size = value.shape[axis]
    if isinstance(shift, int):
        shift = shift % size
        if shift == 0:
            return value
    return pltpu.roll(value, shift, axis)


def base_at(x):
    return lax.rem(48 * lax.axis_index("gx") + 12 * x + 80, LANES)


def within(x, first, end, shape):
    place = (lanes_of(shape) + (LANES - base_at(x) - first)) & (LANES - 1)
    return place < end - first


def towards(sign):
    return [c for c in range(NFLOW) if MOVING[c][0] == sign]


def start_kernel(flow_in, species_in, fluid_in, react_in, block_ref, right_ref, left_ref, flow_ref, species_ref, fluid_ref, react_ref, done):
    pairs = ((flow_in, flow_ref), (species_in, species_ref), (fluid_in, fluid_ref), (react_in, react_ref))
    copies = [pltpu.make_async_copy(one, two, done.at[k]) for k, (one, two) in enumerate(pairs)]
    for copy in copies:
        copy.start()
    for copy in copies:
        copy.wait()
    for x in range(DEEP):
        turn = lax.rem(base_at(DEEP + x) + 8, LANES)
        fluid = fluid_ref[x].astype(jnp.float32)
        react = react_ref[x].astype(jnp.float32)
        flow = [flow_ref[k, x] * fluid for k in range(10)]
        species = [species_ref[k, x] * fluid for k in range(4)]
        post = collide(flow, species)
        for far, sign, ref in ((0, 1, right_ref), (3, -1, left_ref)):
            if x == far:
                _, flow_pops = flow_populations(post[:10])
                _, species_pops = species_populations(post[10:])
                parts = [flow_pops[c] for c in towards(sign)] + [species_pops[towards(sign)[0]], fluid]
                parts[0] = jnp.where(fluid > 0.5, parts[0], react)
                for k, value in enumerate(parts):
                    ref[NEAR + k] = roll(value, turn, 1)
        post[0] = jnp.where(fluid > 0.5, post[0], react)
        for k, value in enumerate(post + [fluid]):
            value = roll(value, turn, 1)
            block_ref[k, x] = value
            if x > 0:
                right_ref[3 * k + x - 1] = value
            if x < 3:
                left_ref[3 * k + x] = value


def put_rows(up_ref, down_ref, place, one, two):
    high = rows_of((ROWS, LANES)) >= 4
    two = roll(two, 4, 0)
    up_ref[place] = jnp.where(high, one, two)
    down_ref[place] = jnp.where(high, two, one)


def layer_of(field, x, own_ref, left_ref, right_ref):
    if x < 4:
        return left_ref[3 * field + x - 1]
    if x < 8:
        return own_ref[field, x - 4]
    return right_ref[3 * field + x - 8]


def own_rows_kernel(block_in, block_ref, up_ref, down_ref, done):
    copy = pltpu.make_async_copy(block_in, block_ref, done)
    copy.start()
    copy.wait()
    for field in range(FIELDS):
        for k in range(2):
            put_rows(up_ref, down_ref, 2 * field + k, block_ref[field, k], block_ref[field, k + 2])


def rows_kernel(left_ref, right_ref, own_up, own_down, up_ref, down_ref):
    for k in range(HALF):
        put_rows(up_ref, down_ref, k, left_ref[k], right_ref[k])


TALL = (2 * ROWS, LANES)


def halves(up_ref, down_ref, place):
    low = rows_of((ROWS, LANES)) < 4
    up, down = up_ref[place], down_ref[place]
    return jnp.where(low, down, up), roll(jnp.where(low, up, down), 4, 0)


def layer_of(field, x, own_ref, left_ref, right_ref):
    if x < 4:
        return left_ref[3 * field + x - 1]
    if x < 8:
        return own_ref[field, x - 4]
    return right_ref[3 * field + x - 8]


def rows_beyond(field, own_up, own_down, up_ref, down_ref):
    found = {}
    for k in range(2):
        found[4 + k], found[6 + k] = halves(own_up, own_down, 2 * field + k)
    for k in range(3):
        found[1 + k], found[8 + k] = halves(up_ref, down_ref, 3 * field + k)
    return found


def edges_kernel(own_ref, left_ref, right_ref, own_up, own_down, up_ref, down_ref, edge_ref):
    refs = (own_ref, left_ref, right_ref)
    here = [within(x, 4, 12, (ROWS, LANES)) for x in range(12)]
    for field in range(FIELDS):
        near = jnp.zeros((ROWS, LANES), jnp.float32)
        beyond = near
        for x, value in rows_beyond(field, own_up, own_down, up_ref, down_ref).items():
            near = jnp.where(here[x], layer_of(field, x, *refs), near)
            beyond = jnp.where(here[x], value, beyond)
        if field < 14:
            x, ref = ((0, left_ref), (11, right_ref))[field // 7]
            value = halves(up_ref, down_ref, FAR_ROWS + field % 7)[field // 7]
            near = jnp.where(here[x], ref[NEAR + field % 7], near)
            beyond = jnp.where(here[x], value, beyond)
        edge_ref[field, 0:ROWS] = near
        edge_ref[field, ROWS : 2 * ROWS] = beyond


def marked(first, conc, fluid):
    solid = fluid < 0.5
    mark = jnp.where(first > 0.5, REACTIVE, SOLID)
    return jnp.where(solid, SOLID, first), jnp.where(solid, mark, conc)


def marked_far(parts):
    solid = parts[6] < 0.5
    mark = jnp.where(parts[0] > 0.5, REACTIVE, SOLID)
    return [jnp.where(solid, SOLID, part) for part in parts[:5]] + [jnp.where(solid, mark, parts[5])]


def moved(value, c):
    cx, cy, cz = MOVING[c]
    return roll(roll(value, 12 * cx + cz, 1), cy, 0)


def send(state_ref, sent_ref, x):
    _, flow_pops = flow_populations([state_ref[k, x] for k in range(10)])
    _, species_pops = species_populations([state_ref[k, x] for k in range(10, 14)])
    for c in range(NFLOW):
        sent_ref[c, x] = moved(flow_pops[c], c)
    for c in range(NSPEC):
        sent_ref[NFLOW + c, x] = moved(species_pops[c], c)


def release(arriving_species):
    parts = [value[0:ROWS] for value in arriving_species]
    parts = [jnp.where(is_number(part), SPECIES_WEIGHT - part, 0.0) for part in parts]
    return (parts[0] + parts[1]) + (parts[2] + parts[3]) + (parts[4] + parts[5])


def results(post, flow, species, released):
    fluid = is_number(post[0])
    out = [jnp.where(fluid, value, 0.0) for value in flow + species]
    return out + [jnp.where(post[10] > LARGEST, REACT_RATE * released, 0.0)]


def layers_kernel(
    own_ref, left_ref, right_ref, own_up, own_down, up_ref, down_ref, result_ref, near_ref, far_ref, state, sent
):
    refs = (own_ref, left_ref, right_ref)
    for field in range(FIELDS):
        for x, value in rows_beyond(field, own_up, own_down, up_ref, down_ref).items():
            state[field, x, 0:ROWS] = layer_of(field, x, *refs)
            state[field, x, ROWS : 2 * ROWS] = value
    for x in range(1, 11):
        rho, conc = marked(state[0, x], state[10, x], state[FLUID, x])
        state[0, x] = rho
        state[10, x] = conc
    for side in range(2):
        own = [within(x, 0, 8, TALL) if side else within(x, 8, 16, TALL) for x in range(1, 11)]
        for field in range(14):
            near = jnp.full(TALL, SOLID if field in (0, 10) else 0.0, jnp.float32)
            for x in range(1, 11):
                near = jnp.where(own[x - 1], state[field, x], near)
            near_ref[side, field] = near
    beyond = [halves(up_ref, down_ref, FAR_ROWS + k) for k in range(7)]
    for end, (x, sign, ref) in enumerate(((0, 1, left_ref), (11, -1, right_ref))):
        parts = marked_far([jnp.concatenate([ref[NEAR + k], beyond[k][end]]) for k in range(7)])
        along = towards(sign)
        for k, c in enumerate(along):
            sent[c, x] = moved(parts[k], c)
        sent[NFLOW + along[0], x] = moved(parts[5], along[0])
        for k in range(6):
            far_ref[end, k] = parts[k]
    released = [jnp.zeros((ROWS, LANES), jnp.float32)] * DEEP
    for step in range(STEPS):
        last = step == STEPS - 1
        for x in range(max(step, 1), 12 - max(step, 1)):
            send(state, sent, x)
        height = ROWS if last else 2 * ROWS
        for x in range(step + 1, 11 - step):
            post = [state[k, x, 0:height] for k in range(14)]
            arriving = [sent[c, x - MOVING[c][0], 0:height] for c in range(NFLOW)]
            arriving_species = [sent[NFLOW + c, x - MOVING[c][0], 0:height] for c in range(NSPEC)]
            new_flow, new_species = pass_on(post, arriving, arriving_species)
            own = x - DEEP
            if 0 <= own < DEEP:
                released[own] = released[own] + release(arriving_species)
            if last:
                for k, value in enumerate(results(post, new_flow, new_species, released[own])):
                    result_ref[k, own] = value
            else:
                for k, value in enumerate(next_post(post, new_flow, new_species)):
                    state[k, x] = value


def strips_kernel(result_ref, near_ref, far_ref, above_ref, below_ref, flow_out, species_out, dissolved_out, strips):
    firsts, posts, fars = (4, 0), [], []
    for side, ref in enumerate((below_ref, above_ref)):
        place = (lanes_of(TALL) + (LANES - base_at(1) - firsts[side])) & (LANES - 1)
        place = place - 12 * ((place * 43) >> 9)
        outside = place >= 8 if side else place < 4
        rho, conc = marked(ref[0], ref[10], ref[FLUID])
        marks = {0: rho, 10: conc}
        posts.append([jnp.where(outside, marks[k] if k in marks else ref[k], near_ref[side, k]) for k in range(14)])
        for end, x in enumerate((0, 11)):
            there = within(x, 8, 12, TALL) if side else within(x, 4, 8, TALL)
            parts = marked_far([ref[7 * end + k] for k in range(7)])
            fars.append([jnp.where(there, part, far_ref[end, k]) for k, part in enumerate(parts)])
    released = [jnp.zeros((ROWS, LANES), jnp.float32)] * 2
    for step in range(STEPS):
        last = step == STEPS - 1
        for side in range(2):
            post = posts[side]
            _, flow_pops = flow_populations(post[:10])
            _, species_pops = species_populations(post[10:])
            arriving = [moved(flow_pops[c], c) for c in range(NFLOW)]
            arriving_species = [moved(species_pops[c], c) for c in range(NSPEC)]
            if step == 0:
                for end, (x, sign) in enumerate(((0, 1), (11, -1))):
                    here = within(x + sign, firsts[side], firsts[side] + 12, TALL)
                    parts = fars[2 * side + end]
                    for k, c in enumerate(towards(sign)):
                        arriving[c] = jnp.where(here, moved(parts[k], c), arriving[c])
                    c = towards(sign)[0]
                    arriving_species[c] = jnp.where(here, moved(parts[5], c), arriving_species[c])
            released[side] = released[side] + release(arriving_species)
            if last:
                post = [value[0:ROWS] for value in post]
                arriving = [value[0:ROWS] for value in arriving]
                arriving_species = [value[0:ROWS] for value in arriving_species]
            new_flow, new_species = pass_on(post, arriving, arriving_species)
            if last:
                for k, value in enumerate(results(post, new_flow, new_species, released[side])):
                    strips[side, k] = value
            else:
                posts[side] = next_post(post, new_flow, new_species)
    for own in range(DEEP):
        x = DEEP + own
        low, high = within(x, 8, 12, (ROWS, LANES)), within(x, 4, 8, (ROWS, LANES))
        back = lax.rem(2 * LANES - 8 - base_at(x), LANES)
        for k in range(15):
            value = jnp.where(low, strips[0, k], jnp.where(high, strips[1, k], result_ref[k, own]))
            value = roll(value, back, 1)
            if k < 10:
                flow_out[k, own] = value
            elif k < 14:
                species_out[k - 10, own] = value
            else:
                dissolved_out[own] = value


def shifted(upward, downward, axis, wrap):
    count = lax.axis_size(axis)
    up = [(i, (i + 1) % count) for i in range(count if wrap else count - 1)]
    down = [(j, i) for i, j in up]
    after = lax.ppermute(downward, axis, down)
    return lax.ppermute(upward, axis, up), after


def vmem(count):
    return [pl.BlockSpec(memory_space=pltpu.VMEM)] * count


def per_device(flow_moments, species_moments, fluid_mask, reactive_mask):
    f32 = jnp.float32
    small = pltpu.CompilerParams(vmem_limit_bytes=16 * 1024 * 1024)
    half = jax.ShapeDtypeStruct((HALF, ROWS, LANES), f32)
    block, to_right, to_left = pl.pallas_call(
        start_kernel,
        out_shape=(jax.ShapeDtypeStruct((FIELDS, DEEP, ROWS, LANES), f32), half, half),
        in_specs=[pl.BlockSpec(memory_space=pltpu.HBM)] * 4,
        out_specs=tuple(vmem(3)),
        scratch_shapes=[
            pltpu.VMEM(flow_moments.shape, f32),
            pltpu.VMEM(species_moments.shape, f32),
            pltpu.VMEM(fluid_mask.shape, fluid_mask.dtype),
            pltpu.VMEM(reactive_mask.shape, reactive_mask.dtype),
            pltpu.SemaphoreType.DMA((4,)),
        ],
        compiler_params=small,
    )(*[pltpu.with_memory_space_constraint(value, pltpu.HBM) for value in (flow_moments, species_moments, fluid_mask, reactive_mask)])
    left, right = shifted(to_right, to_left, "gx", True)
    own_tiles = jax.ShapeDtypeStruct((OWN_TILES, ROWS, LANES), f32)
    block, own_to_up, own_to_down = pl.pallas_call(
        own_rows_kernel,
        out_shape=(jax.ShapeDtypeStruct(block.shape, f32), own_tiles, own_tiles),
        in_specs=[pl.BlockSpec(memory_space=pltpu.HBM)],
        out_specs=tuple(vmem(3)),
        scratch_shapes=[pltpu.SemaphoreType.DMA],
        compiler_params=small,
        cost_estimate=pl.CostEstimate(flops=10**7, bytes_accessed=10**7, transcendentals=0),
    )(block)
    own_rows = shifted(own_to_up, own_to_down, "gy", False)
    tiles = jax.ShapeDtypeStruct((HALF, ROWS, LANES), f32)
    to_up, to_down = pl.pallas_call(
        rows_kernel,
        out_shape=(tiles, tiles),
        in_specs=vmem(2) + [pl.BlockSpec(memory_space=pl.ANY)] * 2,
        out_specs=tuple(vmem(2)),
        compiler_params=small,
    )(left, right, *own_rows)
    rows = own_rows + shifted(to_up, to_down, "gy", False)
    strips = jax.ShapeDtypeStruct((FIELDS,) + TALL, f32)
    edge = pl.pallas_call(
        edges_kernel,
        out_shape=strips,
        in_specs=vmem(7),
        out_specs=vmem(1)[0],
        compiler_params=small,
    )(block, left, right, *rows)
    below, above = shifted(edge, edge, "gz", False)
    result, near, far = pl.pallas_call(
        layers_kernel,
        out_shape=(
            jax.ShapeDtypeStruct((15, DEEP, ROWS, LANES), f32),
            jax.ShapeDtypeStruct((2, 14) + TALL, f32),
            jax.ShapeDtypeStruct((2, 6) + TALL, f32),
        ),
        in_specs=vmem(7),
        out_specs=tuple(vmem(3)),
        scratch_shapes=[
            pltpu.VMEM((FIELDS, 12) + TALL, f32),
            pltpu.VMEM((NFLOW + NSPEC, 12) + TALL, f32),
        ],
        compiler_params=small,
        cost_estimate=pl.CostEstimate(flops=10**7, bytes_accessed=10**7, transcendentals=0),
    )(block, left, right, *rows)
    return pl.pallas_call(
        strips_kernel,
        out_shape=(
            jax.ShapeDtypeStruct(flow_moments.shape, f32),
            jax.ShapeDtypeStruct(species_moments.shape, f32),
            jax.ShapeDtypeStruct(fluid_mask.shape, f32),
        ),
        in_specs=vmem(5),
        out_specs=tuple(vmem(3)),
        scratch_shapes=[pltpu.VMEM((2, 15, ROWS, LANES), f32)],
        compiler_params=small,
    )(result, near, far, above, below)


def solution(mesh):
    return jax.shard_map(
        per_device,
        mesh=mesh,
        in_specs=(
            P(None, "gx", "gy", "gz"),
            P(None, "gx", "gy", "gz"),
            P("gx", "gy", "gz"),
            P("gx", "gy", "gz"),
        ),
        out_specs=(P(None, "gx", "gy", "gz"), P(None, "gx", "gy", "gz"), P("gx", "gy", "gz")),
        check_vma=False,
    )
```
